256 devices in a mesh: gx: 4 (over y_hi, core), gy: 4 (over x), gz: 16 (over y_lo, z).
Axes of the slice: x: 4, y: 4 (y_hi: 2, y_lo: 2; y = y_hi * 2 + y_lo), z: 8, core: 2. Of those that a mesh axis runs over, the one named last changes fastest.
Arguments:
- labels: int32 [32, 48, 2048], P('gx', 'gy', 'gz'), may hold values from 0 to 1
- density_jitter: float32 [2, 32, 48, 2048], P(None, 'gx', 'gy', 'gz'), may hold values from 0.7 to 1.4
- velocity: float32 [3, 32, 48, 2048], P(None, 'gx', 'gy', 'gz'), may hold values from -0.2 to 0.2
Outputs:
- populations: float32 [2, 19, 32, 48, 2048], P(None, None, 'gx', 'gy', 'gz')
The draws below stay inside these ranges and needn't reach their ends.
All inputs are finite; a program needn't handle non-finite values.
Results may differ from the reference program's by a relative error of at most 0.0001.
Values sent between devices are 32-bit elements; how exact they have to be, the bound alone decides.
A program may use at most 192 MiB of HBM per device.

```python
import math
import jax
import jax.numpy as jnp

STEPS = 2
NX = 32
NY = 48
NZ = 2048


def touch_ends(drawn, stream_key, least, largest):
    shape = drawn.shape
    spot = [jax.random.randint(jax.random.fold_in(stream_key, axis), (), 0, shape[axis]) for axis in range(len(shape))]
    drawn = drawn.at[tuple(spot)].set(least)
    longest = shape.index(max(shape))
    spot[longest] = (spot[longest] + 1) % shape[longest]
    return drawn.at[tuple(spot)].set(largest)


def levels(own_key, extent, cuts, low, high):
    loudness = 1.0
    for axis_at, blocks in cuts:
        heights = jax.random.uniform(jax.random.fold_in(jax.random.fold_in(own_key, 6), axis_at), (blocks,), jnp.float32, low / len(cuts), high / len(cuts))
        loudness = loudness * jnp.repeat(jnp.exp(heights), extent[axis_at] // blocks).reshape((-1,) + (1,) * (len(extent) - 1 - axis_at))
    return loudness


def gaussian(own_key, extent, width, bound, cuts=(), held_as=jnp.bfloat16):
    level = levels(own_key, extent, cuts, -0.22, 0.18) if cuts else 1.0
    entries = jax.random.normal(own_key, extent, jnp.float32) * width * level
    return jnp.minimum(jnp.maximum(entries, -bound), bound).astype(held_as)


def setup_inputs(seed: int = 0) -> dict:
    key_of = jax.random.split(jax.random.key(seed), 4)
    labels = touch_ends(jax.random.randint(key_of[0], (NX, NY, NZ), 0, 2), jax.random.fold_in(key_of[0], 1), 0, 1).astype(jnp.int32)
    density_jitter = jnp.clip(jnp.exp(math.log(1.4) - 0.6931472 * jax.random.uniform(key_of[1], (2, NX, NY, NZ), jnp.float32) ** levels(key_of[1], (2, NX, NY, NZ), ((1, 4), (2, 4), (3, 16)), -0.2, 0.2)), 0.7, 1.4)
    velocity = gaussian(key_of[2], (3, NX, NY, NZ), 0.08, 0.2, ((1, 4), (2, 4), (3, 16)), jnp.float32)
    return {"labels": labels, "density_jitter": density_jitter, "velocity": velocity}


VELS = [(0, 0, 0), (1, 0, 0), (-1, 0, 0), (0, 1, 0), (0, -1, 0), (0, 0, 1), (0, 0, -1),
        (1, 1, 0), (-1, -1, 0), (1, -1, 0), (-1, 1, 0), (1, 0, 1), (-1, 0, -1),
        (1, 0, -1), (-1, 0, 1), (0, 1, 1), (0, -1, -1), (0, 1, -1), (0, -1, 1)]
WEIGHTS = [1.0 / 3.0] + [1.0 / 18.0] * 6 + [1.0 / 36.0] * 12
FWEIGHTS = [0.0] + [1.0 / 6.0] * 6 + [1.0 / 12.0] * 12
COUPLE_CROSS = 1.5
COUPLE_SELF = 0.5


def take(field, margin, dx, dy, dz):
    nx = field.shape[-3] - 2 * margin
    ny = field.shape[-2] - 2 * margin
    nz = field.shape[-1] - 2 * margin
    return field[..., margin + dx:margin + dx + nx, margin + dy:margin + dy + ny, margin + dz:margin + dz + nz]


def equilibrium(rho, vel, index):
    cx, cy, cz = VELS[index]
    dotted = cx * vel[0] + cy * vel[1] + cz * vel[2]
    square = vel[0] * vel[0] + vel[1] * vel[1] + vel[2] * vel[2]
    return WEIGHTS[index] * rho * (1.0 + 3.0 * dotted + 4.5 * dotted * dotted - 1.5 * square)


def start_state(rho0, vel):
    return jnp.stack([equilibrium(rho0, vel, index) for index in range(19)], axis=1)


def forces(psi):
    centre = take(psi, 2, 0, 0, 0)
    other = psi[::-1]
    cross = [0.0, 0.0, 0.0]
    same = [0.0, 0.0, 0.0]
    for index in range(1, 19):
        vec = VELS[index]
        near = take(other, 2, vec[0], vec[1], vec[2])
        far = take(psi, 2, 2 * vec[0], 2 * vec[1], 2 * vec[2])
        for comp in range(3):
            if vec[comp] != 0:
                cross[comp] = cross[comp] + FWEIGHTS[index] * vec[comp] * near
                same[comp] = same[comp] + FWEIGHTS[index] * vec[comp] * far
    total = COUPLE_CROSS * jnp.stack(cross, axis=1) + COUPLE_SELF * jnp.stack(same, axis=1)
    return -centre[:, None] * total


def collide(state, force):
    rho = jnp.sum(state, axis=1)
    rho_tot = rho[0] + rho[1]
    vel = []
    for comp in range(3):
        moment = 0.0
        for index in range(1, 19):
            if VELS[index][comp] != 0:
                moment = moment + VELS[index][comp] * (state[0, index] + state[1, index])
        vel.append((moment + 0.5 * (force[0, comp] + force[1, comp])) / rho_tot)
    taus = jnp.array([1.0, 0.8], jnp.float32).reshape(2, 1, 1, 1)
    u_force = vel[0] * force[:, 0] + vel[1] * force[:, 1] + vel[2] * force[:, 2]
    result = []
    for index in range(19):
        cx, cy, cz = VELS[index]
        feq = equilibrium(rho, vel, index)
        dotted = cx * vel[0] + cy * vel[1] + cz * vel[2]
        c_force = cx * force[:, 0] + cy * force[:, 1] + cz * force[:, 2]
        source = WEIGHTS[index] * (1.0 - 0.5 / taus) * (3.0 * (c_force - u_force) + 9.0 * dotted * c_force)
        result.append(state[:, index] - (state[:, index] - feq) / taus + source)
    return jnp.stack(result, axis=1)


def stream(post):
    return jnp.stack([take(post[:, index], 1, -VELS[index][0], -VELS[index][1], -VELS[index][2]) for index in range(19)], axis=1)


def wrap_pad(field, margin):
    widths = [(0, 0)] * (field.ndim - 3) + [(margin, margin)] * 3
    return jnp.pad(field, widths, mode="wrap")


def initial_density(labels, density_jitter):
    droplet = labels == 1
    first = jnp.where(droplet, 2.0, 0.15).astype(jnp.float32) * density_jitter[0]
    second = jnp.where(droplet, 0.15, 2.0).astype(jnp.float32) * density_jitter[1]
    return jnp.stack([first, second], axis=0)


def reference(labels, density_jitter, velocity):
    rho0 = initial_density(labels, density_jitter)
    state = start_state(rho0, velocity)
    for step in range(STEPS):
        psi = 1.0 - jnp.exp(-jnp.sum(state, axis=1))
        force = forces(wrap_pad(psi, 2))
        post = collide(state, force)
        state = stream(wrap_pad(post, 1))
    return state
```

```python
import functools
import itertools

import jax
import jax.numpy as jnp
from jax import lax
from jax.experimental import pallas as pl
from jax.experimental.pallas import tpu as pltpu
from jax.sharding import PartitionSpec as P

MESH = pl.DeviceIdType.MESH
F32 = jnp.float32
VELS = [(0, 0, 0), (1, 0, 0), (-1, 0, 0), (0, 1, 0), (0, -1, 0), (0, 0, 1), (0, 0, -1),
        (1, 1, 0), (-1, -1, 0), (1, -1, 0), (-1, 1, 0), (1, 0, 1), (-1, 0, -1),
        (1, 0, -1), (-1, 0, 1), (0, 1, 1), (0, -1, -1), (0, 1, -1), (0, -1, 1)]
TAU_INV = (1.0, 1.25)
SRC = (0.5, 0.375)
GROUPS = [(a, b) for a in (-1, 0, 1) for b in (-1, 0, 1)]
ZGROUPS = [(0, 0), (1, 0), (-1, 0), (0, 1), (0, -1)]
NEIGHBOURS = [d for d in itertools.product((-1, 0, 1), repeat=3) if d != (0, 0, 0)]
EXCHANGED = [(2, 2, 48, 128), (3, 3, 32, 128), (2, 2, 2, 8, 128),
             (2, 2, 2, 40, 128), (2, 3, 3, 16, 128),
             (2, 2, 48, 128), (2, 3, 32, 128),
             (2, 2, 2, 40, 128), (2, 2, 3, 16, 128),
             (2, 3, 2, 2, 8, 128), (2, 3, 2, 2, 8, 128)]


def lane_of(rows):
    return lax.broadcasted_iota(jnp.int32, (rows, 128), 1)


def lroll(v, k):
    k = k % 128
    return v if isinstance(k, int) and k == 0 else pltpu.roll(v, k, 1)


def yroll(v, k):
    k = k % v.shape[0]
    return v if k == 0 else pltpu.roll(v, k, 0)


def z_place(f, x):
    if f < 2:
        return 0, 48 * f + 6 * x
    if f < 4:
        return 1, 48 * (f - 2) + 6 * x
    return (0, 96 + 6 * x) if x < 4 else (1, 96 + 6 * (x - 4))


def exchange_kernel(lab_ref, jit_ref, vel_ref, ro, uo, zp, rx, ux, ry, uy, re, ue, zf, ze,
                    labv, jitv, velv, lsem, ssem, rsem):
    ix, iy, iz = lax.axis_index("gx"), lax.axis_index("gy"), lax.axis_index("gz")
    nx, ny, nz = lax.axis_size("gx"), lax.axis_size("gy"), lax.axis_size("gz")

    def device(d):
        return (lax.rem(ix + d[0] + nx, nx), lax.rem(iy + d[1] + ny, ny), lax.rem(iz + d[2] + nz, nz))

    barrier = pltpu.get_barrier_semaphore()
    for d in NEIGHBOURS:
        pl.semaphore_signal(barrier, inc=1, device_id=device(d), device_id_type=MESH)
    loads = [pltpu.make_async_copy(a, b, lsem.at[n]) for n, (a, b) in
             enumerate(((lab_ref, labv), (jit_ref, jitv), (vel_ref, velv)))]
    for load in loads:
        load.start()
    for load in loads:
        load.wait()
    for x in range(8):
        drop = labv[x] == 1
        jitv[0, x] = jnp.where(drop, 2.0, 0.15).astype(F32) * jitv[0, x]
        jitv[1, x] = jnp.where(drop, 0.15, 2.0).astype(F32) * jitv[1, x]
    lane = lane_of(6)
    for h in range(2):
        packs = [[jnp.zeros((6, 128), F32) for _ in range(2)] for _ in range(2)]
        for f in range(5):
            for x in range(8):
                val = (jitv[f, x, 6 * h:6 * h + 6, :] if f < 2 else velv[f - 2, x, 6 * h:6 * h + 6, :])
                if f < 2:
                    ro[f, h, 6 * x:6 * x + 6, :] = val
                k, l0 = z_place(f, x)
                here = (lane >= l0) & (lane < l0 + 6)
                packs[0][k] = jnp.where(here, lroll(val, l0), packs[0][k])
                packs[1][k] = jnp.where(here, lroll(val, l0 + 6), packs[1][k])
        for zs in range(2):
            for k in range(2):
                zp[zs, h, k, 0:6, :] = packs[zs][k]
                zp[zs, h, k, 6:8, :] = packs[zs][k][0:2]
    for f in range(3):
        for g in range(3):
            for x in range(8):
                uo[f, g, 4 * x:4 * x + 4, :] = velv[f, x, 4 * g:4 * g + 4, :]
    pl.semaphore_wait(barrier, len(NEIGHBOURS))

    copies = []

    def send(src, dst, d):
        n = len(copies)
        copy = pltpu.make_async_remote_copy(src_ref=src, dst_ref=dst, send_sem=ssem.at[n], recv_sem=rsem.at[n],
                                            device_id=device(d), device_id_type=MESH)
        copy.start()
        copies.append(copy)

    for dz in (1, -1):
        zs_mine, zs_theirs = (1, 0) if dz == 1 else (0, 1)
        for dx in (0, 1, -1):
            send(zp.at[zs_mine], zf.at[zs_theirs, 1 - dx], (dx, 0, dz))
            for dy in (1, -1):
                h, side = (1, 0) if dy == 1 else (0, 1)
                send(zp.at[zs_mine, h], ze.at[zs_theirs, 1 - dx, side], (dx, dy, dz))
    for dx in (1, -1):
        sx, r0, u0 = (0, 8, 16) if dx == 1 else (1, 0, 0)
        send(ro.at[:, :, r0:r0 + 40], rx.at[sx], (dx, 0, 0))
        send(uo.at[:, :, u0:u0 + 16], ux.at[sx], (dx, 0, 0))
        for dy in (1, -1):
            sy, h, g = (0, 1, 2) if dy == 1 else (1, 0, 0)
            send(ro.at[:, h, r0:r0 + 40], re.at[sx, sy], (dx, dy, 0))
            send(uo.at[:, g, u0:u0 + 16], ue.at[sx, sy], (dx, dy, 0))
    for dy in (1, -1):
        sy, h, g = (0, 1, 2) if dy == 1 else (1, 0, 0)
        send(ro.at[:, h], ry.at[sy], (0, dy, 0))
        send(uo.at[:, g], uy.at[sy], (0, dy, 0))
    for copy in copies:
        copy.wait()


def exchange(labels, jitter, velocity):
    any_spec = pl.BlockSpec(memory_space=pl.ANY)
    vmem = pl.BlockSpec(memory_space=pltpu.VMEM)
    return pl.pallas_call(
        exchange_kernel,
        out_shape=[jax.ShapeDtypeStruct(s, F32) for s in EXCHANGED],
        in_specs=[any_spec] * 3,
        out_specs=[vmem] * len(EXCHANGED),
        scratch_shapes=[pltpu.VMEM((8, 12, 128), jnp.int32), pltpu.VMEM((2, 8, 12, 128), F32),
                        pltpu.VMEM((3, 8, 12, 128), F32), pltpu.SemaphoreType.DMA((3,)),
                        pltpu.SemaphoreType.DMA((34,)), pltpu.SemaphoreType.DMA((34,))],
        compiler_params=pltpu.CompilerParams(collective_id=0, has_side_effects=True, vmem_limit_bytes=16 << 20),
    )(labels, jitter, velocity)


NS1, NP1, NS2 = 34, 26, 28


def stage_a(src, slab, rho_is, fields):
    for s in range(2):
        p = 1.0 - jnp.exp(-src[s, slab])
        fields[s, 0, slab] = p
        for n, (k, c6, c12) in enumerate(((1, 0.25, 0.125), (2, 0.5 / 6, 0.5 / 12))):
            up, down = lroll(p, -k), lroll(p, k)
            bz = c6 * p + c12 * (up + down)
            dz = c12 * (up - down)
            fields[s, 1 + n, slab] = bz + c12 * (yroll(p, k) + yroll(p, -k))
            fields[s, 3 + n, slab] = bz
            fields[s, 5 + n, slab] = 2.0 * dz + (yroll(dz, k) + yroll(dz, -k))
            fields[s, 7 + n, slab] = dz


def force(fields, slab, rows):
    near, far = [], []
    for s in range(2):
        for n, (k, c12, out) in enumerate(((1, 0.125, near), (2, 0.5 / 12, far))):
            gx = fields[s, 1 + n, slab + k, 0:rows] - fields[s, 1 + n, slab - k, 0:rows]
            by = fields[s, 3 + n, slab] + c12 * (fields[s, 0, slab + k] + fields[s, 0, slab - k])
            gy = (yroll(by, -k) - yroll(by, k))[0:rows]
            gz = fields[s, 5 + n, slab, 0:rows] + (fields[s, 7 + n, slab + k, 0:rows] + fields[s, 7 + n, slab - k, 0:rows])
            out.append((gx, gy, gz))
    result = []
    for s in range(2):
        minus = -fields[s, 0, slab, 0:rows]
        result.append([minus * (near[1 - s][a] + far[s][a]) for a in range(3)])
    return result


def populations(s, rho, v, f, old=None):
    w = 1.0 / 36.0
    rt = (w * TAU_INV[s]) * rho
    vv = v[0] * v[0] + v[1] * v[1] + v[2] * v[2]
    vf = v[0] * f[0] + v[1] * f[1] + v[2] * f[2]
    a0 = rt * (1.0 - 1.5 * vv) - (3.0 * SRC[s] * w) * vf
    b = [3.0 * (rt * v[a] + (SRC[s] * w) * f[a]) for a in range(3)]
    g = [4.5 * rt * v[a] + (9.0 * SRC[s] * w) * f[a] for a in range(3)]
    diag = [v[a] * g[a] for a in range(3)]
    off = {(a, c): v[a] * g[c] + v[c] * g[a] for a, c in ((0, 1), (0, 2), (1, 2))}
    if old is not None:
        part = 1.0 - TAU_INV[s]
        ro = (w * part) * rho
        uu = old[0] * old[0] + old[1] * old[1] + old[2] * old[2]
        a0 = a0 + ro * (1.0 - 1.5 * uu)
        h = [4.5 * ro * old[a] for a in range(3)]
        b = [b[a] + 3.0 * ro * old[a] for a in range(3)]
        diag = [diag[a] + old[a] * h[a] for a in range(3)]
        off = {(a, c): off[a, c] + 2.0 * (old[a] * h[c]) for a, c in off}
    post = {(0, 0, 0): 12.0 * a0}
    for a in range(3):
        even, odd = a0 + diag[a], b[a]
        unit = [0, 0, 0]
        unit[a] = 1
        post[tuple(unit)] = 2.0 * (even + odd)
        post[tuple(-q for q in unit)] = 2.0 * (even - odd)
    for a, c in off:
        base = a0 + (diag[a] + diag[c])
        for sign in (1, -1):
            even = base + off[a, c] if sign == 1 else base - off[a, c]
            odd = b[a] + b[c] if sign == 1 else b[a] - b[c]
            unit = [0, 0, 0]
            unit[a], unit[c] = 1, sign
            post[tuple(unit)] = even + odd
            post[tuple(-q for q in unit)] = even - odd
    return post


def compute_kernel(ro, uo, zp, rx, ux, ry, uy, re, ue, zf, ze, out_ref,
                   rho, vel, zr, fld, pops, qs, qz, rho1, mom, fld1, sout, outx, sem):
    for e in range(20):
        dx, x = (0, e + 2) if e < 6 else (1, e - 6) if e < 14 else (2, e - 14)
        for c in range(2):
            for j in range(4):
                if dx == 1:
                    r0 = 6 * x
                    part = (ry[0, c, r0:r0 + 6] if j == 0 else ry[1, c, r0:r0 + 6] if j == 3 else
                            ro[c, j - 1, r0:r0 + 6])
                else:
                    sx = dx // 2
                    r0 = 6 * x - (8 if sx == 0 else 0)
                    part = (re[sx, 0, c, r0:r0 + 6] if j == 0 else re[sx, 1, c, r0:r0 + 6] if j == 3 else
                            rx[sx, c, j - 1, r0:r0 + 6])
                rho[c, e, 6 * j:6 * j + 6, :] = part
    for k in range(16):
        dx, x = (0, k + 4) if k < 4 else (1, k - 4) if k < 12 else (2, k - 12)
        for f in range(3):
            for j in range(5):
                if dx == 1:
                    r0 = 4 * x
                    part = (uy[0, f, r0:r0 + 4] if j == 0 else uy[1, f, r0:r0 + 4] if j == 4 else
                            uo[f, j - 1, r0:r0 + 4])
                else:
                    sx = dx // 2
                    r0 = 4 * x - (16 if sx == 0 else 0)
                    part = (ue[sx, 0, f, r0:r0 + 4] if j == 0 else ue[sx, 1, f, r0:r0 + 4] if j == 4 else
                            ux[sx, f, j - 1, r0:r0 + 4])
                vel[f, k, 2 + 4 * j:6 + 4 * j, :] = part
    for zs in range(2):
        for dx in range(3):
            for k in range(2):
                zr[zs, dx, k, 0:6] = ze[zs, dx, 0, k, 0:6]
                zr[zs, dx, k, 6:12] = zf[zs, dx, 0, k, 0:6]
                zr[zs, dx, k, 12:18] = zf[zs, dx, 1, k, 0:6]
                zr[zs, dx, k, 18:24] = ze[zs, dx, 1, k, 0:6]
    lane = lane_of(24)
    in_seg = lane % 18
    for f in range(5):
        merged = []
        for zs in range(2):
            m = jnp.zeros((24, 128), F32)
            for dx, (e_lo, e_hi) in enumerate(((0, 6), (6, 14), (14, 20))):
                off = 6 + 8 * (dx - 1)
                for x_lo, x_hi in ((0, 4), (4, 8)) if f == 4 else ((0, 8),):
                    a, b = max(e_lo, x_lo + off), min(e_hi, x_hi + off)
                    if a >= b:
                        continue
                    tile, l0 = z_place(f, x_lo)
                    shift = 6 * (x_lo + off) - l0
                    m = jnp.where((lane >= 6 * a) & (lane < 6 * b), lroll(zr[zs, dx, tile], shift), m)
            merged.append(m)
        for xo in range(3):
            low = lroll(merged[0], -6 * xo)
            high = lroll(merged[1], 6 - 6 * xo)
            for seg in range(7):
                e = 3 * seg + xo
                if f < 2:
                    if e > 19:
                        continue
                    val = rho[f, e]
                else:
                    if e < 2 or e > 17:
                        continue
                    val = vel[f - 2, e - 2]
                val = lroll(val, 18 * seg + 6)
                low = jnp.where((lane >= 18 * seg + 6) & (lane < 18 * seg + 18), val, low)
                start = (18 * seg - 6) % 128
                if seg == 0:
                    high = jnp.where((lane >= 122) | (lane < 6), val, high)
                else:
                    high = jnp.where((lane >= start) & (lane < start + 12), val, high)
            if f < 2:
                for base, v in ((20, low), (27, high)):
                    rho[f, base + 2 + xo] = v
                    if xo == 0:
                        rho[f, base + 5] = lroll(v, -18)
                    if xo == 1:
                        rho[f, base] = lroll(v, 18)
                        rho[f, base + 6] = lroll(v, -18)
                    if xo == 2:
                        rho[f, base + 1] = lroll(v, 18)
            else:
                vel[f - 2, 16 + xo] = low
                vel[f - 2, 19 + xo] = high

    @pl.loop(0, NS1)
    def _(slab):
        stage_a(rho, slab, None, fld)

    @pl.loop(0, 22)
    def _(j):
        late, later = (j >= 16).astype(jnp.int32), (j >= 19).astype(jnp.int32)
        slab = j + 2 + 4 * late + 4 * later
        dst = j + late + 2 * later
        fs = force(fld, slab, 24)
        r = [rho[s, slab] for s in range(2)]
        u = [vel[a, j] for a in range(3)]
        half = 0.5 / (r[0] + r[1])
        v = [u[a] + half * (fs[0][a] + fs[1][a]) for a in range(3)]
        zsum = {}
        for s in range(2):
            post = populations(s, r[s], v, fs[s], u if s == 1 else None)
            sums = {}
            for i, (cx, cy, cz) in enumerate(VELS):
                val = lroll(post[VELS[i]], cz)
                if s == 1:
                    pops[i, dst, 8:32] = val
                sums[cx, cy] = val if (cx, cy) not in sums else sums[cx, cy] + val
                if cz:
                    part = val if cz == 1 else -val
                    zsum[cx, cy] = part if (cx, cy) not in zsum else zsum[cx, cy] + part
            for n, key in enumerate(GROUPS):
                qs[s, n, dst, 8:32] = sums[key]
        for n, key in enumerate(ZGROUPS):
            qz[n, dst, 8:32] = zsum[key]

    for base in (16, 21):
        for n, (cx, cy) in enumerate(GROUPS):
            for s in range(2):
                if cx == 1:
                    qs[s, n, base, 8:32] = lroll(qs[s, n, base + 3, 8:32], 18)
                if cx == -1:
                    qs[s, n, base + 4, 8:32] = lroll(qs[s, n, base + 1, 8:32], -18)
        for n, (cx, cy) in enumerate(ZGROUPS):
            if cx == 1:
                qz[n, base, 8:32] = lroll(qz[n, base + 3, 8:32], 18)
            if cx == -1:
                qz[n, base + 4, 8:32] = lroll(qz[n, base + 1, 8:32], -18)
        for i, (cx, cy, cz) in enumerate(VELS):
            if cx == 1:
                pops[i, base, 8:32] = lroll(pops[i, base + 3, 8:32], 18)
            if cx == -1:
                pops[i, base + 4, 8:32] = lroll(pops[i, base + 1, 8:32], -18)

    @pl.loop(0, 20)
    def _(g):
        late, later = (g >= 14).astype(jnp.int32), (g >= 17).astype(jnp.int32)
        src = g + 1 + 2 * late + 2 * later
        dst = g + 2 * late + 4 * later
        mx = my = 0.0
        for s in range(2):
            top = bottom = 0.0
            for n, (cx, cy) in enumerate(GROUPS):
                a = qs[s, n, src - cx, 13 - cy:29 - cy]
                top = top + a
                bottom = bottom + qs[s, n, src - cx, 5 - cy:13 - cy]
                mx = mx + cx * a if cx else mx
                my = my + cy * a if cy else my
            rho1[s, dst, 0:16] = top
            rho1[s, dst, 16:24] = bottom
        mz = 0.0
        for n, (cx, cy) in enumerate(ZGROUPS):
            mz = mz + qz[n, src - cx, 13 - cy:29 - cy]
        mom[0, dst], mom[1, dst], mom[2, dst] = mx, my, mz

    for base in (14, 21):
        for s in range(2):
            rho1[s, base] = lroll(rho1[s, base + 3], 18)
            rho1[s, base + 1] = lroll(rho1[s, base + 4], 18)
            rho1[s, base + 5] = lroll(rho1[s, base + 2], -18)
            rho1[s, base + 6] = lroll(rho1[s, base + 3], -18)

    @pl.loop(0, NS2)
    def _(slab):
        stage_a(rho1, slab, None, fld1)

    def second(slab, src, write):
        fs = force(fld1, slab, 16)
        r = [rho1[s, slab, 0:16] for s in range(2)]
        inv = 1.0 / (r[0] + r[1])
        v = [(mom[a, slab] + 0.5 * (fs[0][a] + fs[1][a])) * inv for a in range(3)]
        for s in range(2):
            post = populations(s, r[s], v, fs[s])
            for i, (cx, cy, cz) in enumerate(VELS):
                val = post[VELS[i]]
                if s == 1:
                    val = val - 0.25 * pops[i, src - cx, 13 - cy:29 - cy]
                write(s, i, yroll(lroll(val, cz), cy - 1))

    @pl.loop(0, 6)
    def _(t):
        later = (t >= 3).astype(jnp.int32)

        def write(s, i, val):
            sout[s, i, t] = val

        second(16 + t + 4 * later, 17 + t + 2 * later, write)

    lane16 = lane_of(16)
    seg16 = lane16 % 18
    from_low = (seg16 >= 6) & (seg16 < 12)
    edge = (lane16 < 6) | (lane16 >= 122)

    @pl.loop(0, 10)
    def _(k):
        e = k + 5
        seg = e // 3
        xo = e - 3 * seg
        shift = lax.rem(256 - 18 * seg - 6, 128)

        def write(s, i, val):
            cx = VELS[i][0]
            strip = jnp.where(from_low, sout[s, i, xo], sout[s, i, xo + 3])
            val = jnp.where(edge, pltpu.roll(strip, shift, 1), val)
            outx[s, i, k + 1 + cx] = val[0:12]

        second(k + 2, k + 3, write)

    copy = pltpu.make_async_copy(outx.at[:, :, 2:10], out_ref, sem.at[0])
    copy.start()
    copy.wait()


def compute(parts):
    vmem = pl.BlockSpec(memory_space=pltpu.VMEM)
    return pl.pallas_call(
        compute_kernel,
        out_shape=jax.ShapeDtypeStruct((2, 19, 8, 12, 128), F32),
        in_specs=[vmem] * len(parts),
        out_specs=pl.BlockSpec(memory_space=pl.ANY),
        scratch_shapes=[
            pltpu.VMEM((2, NS1, 24, 128), F32), pltpu.VMEM((3, 22, 24, 128), F32), pltpu.VMEM((2, 3, 2, 24, 128), F32),
            pltpu.VMEM((2, 9, NS1, 24, 128), F32), pltpu.VMEM((19, NP1, 40, 128), F32),
            pltpu.VMEM((2, 9, NP1, 40, 128), F32), pltpu.VMEM((5, NP1, 40, 128), F32),
            pltpu.VMEM((2, NS2, 24, 128), F32), pltpu.VMEM((3, NS2, 16, 128), F32),
            pltpu.VMEM((2, 9, NS2, 24, 128), F32), pltpu.VMEM((2, 19, 6, 16, 128), F32),
            pltpu.VMEM((2, 19, 12, 12, 128), F32), pltpu.SemaphoreType.DMA((1,))],
        compiler_params=pltpu.CompilerParams(vmem_limit_bytes=58 << 20),
    )(*parts)


def local(labels, density_jitter, velocity):
    return compute(exchange(labels, density_jitter, velocity))


def solution(mesh):
    in_specs = (P("gx", "gy", "gz"), P(None, "gx", "gy", "gz"), P(None, "gx", "gy", "gz"))
    out_specs = P(None, None, "gx", "gy", "gz")
    return jax.shard_map(local, mesh=mesh, in_specs=in_specs, out_specs=out_specs, check_vma=False)
```

```python
import functools
import itertools

import jax
import jax.numpy as jnp
from jax import lax
from jax.experimental import pallas as pl
from jax.experimental.pallas import tpu as pltpu
from jax.sharding import PartitionSpec as P

MESH = pl.DeviceIdType.MESH
F32 = jnp.float32
VELS = [(0, 0, 0), (1, 0, 0), (-1, 0, 0), (0, 1, 0), (0, -1, 0), (0, 0, 1), (0, 0, -1),
        (1, 1, 0), (-1, -1, 0), (1, -1, 0), (-1, 1, 0), (1, 0, 1), (-1, 0, -1),
        (1, 0, -1), (-1, 0, 1), (0, 1, 1), (0, -1, -1), (0, 1, -1), (0, -1, 1)]
TAU_INV = (1.0, 1.25)
SRC = (0.5, 0.375)
GROUPS = [(a, b) for a in (-1, 0, 1) for b in (-1, 0, 1)]
ZGROUPS = [(0, 0), (1, 0), (-1, 0), (0, 1), (0, -1)]
NEIGHBOURS = [d for d in itertools.product((-1, 0, 1), repeat=3) if d != (0, 0, 0)]
EXCHANGED = [(2, 2, 48, 128), (3, 3, 32, 128), (2, 2, 2, 8, 128),
             (2, 2, 2, 40, 128), (2, 3, 3, 16, 128),
             (2, 2, 48, 128), (2, 3, 32, 128),
             (2, 2, 2, 40, 128), (2, 2, 3, 16, 128),
             (2, 3, 2, 2, 8, 128), (2, 3, 2, 2, 8, 128)]


def lane_of(rows):
    return lax.broadcasted_iota(jnp.int32, (rows, 128), 1)


def lroll(v, k):
    k = k % 128
    return v if isinstance(k, int) and k == 0 else pltpu.roll(v, k, 1)


def yroll(v, k):
    k = k % v.shape[0]
    return v if k == 0 else pltpu.roll(v, k, 0)


def z_place(f, x):
    if f < 2:
        return 0, 48 * f + 6 * x
    if f < 4:
        return 1, 48 * (f - 2) + 6 * x
    return (0, 96 + 6 * x) if x < 4 else (1, 96 + 6 * (x - 4))


def exchange_kernel(lab_ref, jit_ref, vel_ref, ro, uo, zp, rx, ux, ry, uy, re, ue, zf, ze,
                    labv, jitv, velv, lsem, ssem, rsem, below):
    ix, iy, iz = lax.axis_index("gx"), lax.axis_index("gy"), lax.axis_index("gz")
    nx, ny, nz = lax.axis_size("gx"), lax.axis_size("gy"), lax.axis_size("gz")

    def device(d):
        return (lax.rem(ix + d[0] + nx, nx), lax.rem(iy + d[1] + ny, ny), lax.rem(iz + d[2] + nz, nz))

    barrier = pltpu.get_barrier_semaphore()
    for d in NEIGHBOURS:
        if d[2] <= 0:
            pl.semaphore_signal(barrier, inc=1, device_id=device(d), device_id_type=MESH)
    loads = [pltpu.make_async_copy(a, b, lsem.at[n]) for n, (a, b) in
             enumerate(((lab_ref, labv), (jit_ref, jitv), (vel_ref, velv)))]
    for load in loads:
        load.start()
    for load in loads:
        load.wait()
    drop = labv[...] == 1
    jitv[0] = jnp.where(drop, 2.0, 0.15).astype(F32) * jitv[0]
    jitv[1] = jnp.where(drop, 0.15, 2.0).astype(F32) * jitv[1]
    lane = lane_of(6)
    for h in range(2):
        packs = [[jnp.zeros((6, 128), F32) for _ in range(2)] for _ in range(2)]
        for f in range(5):
            for x in range(8):
                rows = pl.ds(48 * h + x, 6, stride=8)
                val = jitv[f, rows, :] if f < 2 else velv[f - 2, rows, :]
                if f < 2:
                    ro[f, h, 6 * x:6 * x + 6, :] = val
                k, l0 = z_place(f, x)
                here = (lane >= l0) & (lane < l0 + 6)
                packs[0][k] = jnp.where(here, lroll(val, l0), packs[0][k])
                packs[1][k] = jnp.where(here, lroll(val, l0 + 6), packs[1][k])
        for zs in range(2):
            for k in range(2):
                zp[zs, h, k, 0:6, :] = packs[zs][k]
                zp[zs, h, k, 6:8, :] = packs[zs][k][0:2]
    for f in range(3):
        for g in range(3):
            for x in range(8):
                uo[f, g, 4 * x:4 * x + 4, :] = velv[f, pl.ds(32 * g + x, 4, stride=8), :]
    pl.semaphore_wait(barrier, 17)
    for d in NEIGHBOURS:
        if d[2] == 1:
            pl.semaphore_signal(below, inc=1, device_id=device(d), device_id_type=MESH)

    copies = []

    def send(src, dst, d):
        n = len(copies)
        copy = pltpu.make_async_remote_copy(src_ref=src, dst_ref=dst, send_sem=ssem.at[n], recv_sem=rsem.at[n],
                                            device_id=device(d), device_id_type=MESH)
        copy.start()
        copies.append(copy)

    def send_z(dz):
        zs_mine, zs_theirs = (1, 0) if dz == 1 else (0, 1)
        for dx in (0, 1, -1):
            send(zp.at[zs_mine], zf.at[zs_theirs, 1 - dx], (dx, 0, dz))
            for dy in (1, -1):
                h, side = (1, 0) if dy == 1 else (0, 1)
                send(zp.at[zs_mine, h], ze.at[zs_theirs, 1 - dx, side], (dx, dy, dz))

    send_z(1)
    for dx in (1, -1):
        sx, r0, u0 = (0, 8, 16) if dx == 1 else (1, 0, 0)
        send(ro.at[:, :, r0:r0 + 40], rx.at[sx], (dx, 0, 0))
        send(uo.at[:, :, u0:u0 + 16], ux.at[sx], (dx, 0, 0))
        for dy in (1, -1):
            sy, h, g = (0, 1, 2) if dy == 1 else (1, 0, 0)
            send(ro.at[:, h, r0:r0 + 40], re.at[sx, sy], (dx, dy, 0))
            send(uo.at[:, g, u0:u0 + 16], ue.at[sx, sy], (dx, dy, 0))
    for dy in (1, -1):
        sy, h, g = (0, 1, 2) if dy == 1 else (1, 0, 0)
        send(ro.at[:, h], ry.at[sy], (0, dy, 0))
        send(uo.at[:, g], uy.at[sy], (0, dy, 0))
    pl.semaphore_wait(below, 9)
    send_z(-1)
    for copy in copies:
        copy.wait()


def exchange(labels, jitter, velocity):
    hbm = pl.BlockSpec(memory_space=pltpu.HBM)
    vmem = pl.BlockSpec(memory_space=pltpu.VMEM)
    return pl.pallas_call(
        exchange_kernel,
        out_shape=[jax.ShapeDtypeStruct(s, F32) for s in EXCHANGED],
        in_specs=[hbm] * 3,
        out_specs=[vmem] * len(EXCHANGED),
        scratch_shapes=[pltpu.VMEM((96, 128), jnp.int32), pltpu.VMEM((2, 96, 128), F32),
                        pltpu.VMEM((3, 96, 128), F32), pltpu.SemaphoreType.DMA((3,)),
                        pltpu.SemaphoreType.DMA((34,)), pltpu.SemaphoreType.DMA((34,)), pltpu.SemaphoreType.REGULAR],
        compiler_params=pltpu.CompilerParams(collective_id=0, has_side_effects=True, vmem_limit_bytes=8 << 20),
    )(labels, jitter, velocity)


NS1, NP1, NS2 = 34, 26, 28


def stage_a(src, slab, rho_is, fields):
    for s in range(2):
        p = 1.0 - jnp.exp(-src[s, slab])
        fields[s, 0, slab] = p
        for n, (k, c6, c12) in enumerate(((1, 0.25, 0.125), (2, 0.5 / 6, 0.5 / 12))):
            up, down = lroll(p, -k), lroll(p, k)
            bz = c6 * p + c12 * (up + down)
            dz = c12 * (up - down)
            fields[s, 1 + n, slab] = bz + c12 * (yroll(p, k) + yroll(p, -k))
            fields[s, 3 + n, slab] = bz
            fields[s, 5 + n, slab] = 2.0 * dz + (yroll(dz, k) + yroll(dz, -k))
            fields[s, 7 + n, slab] = dz


def force(fields, slab, rows):
    near, far = [], []
    for s in range(2):
        for n, (k, c12, out) in enumerate(((1, 0.125, near), (2, 0.5 / 12, far))):
            gx = fields[s, 1 + n, slab + k, 0:rows] - fields[s, 1 + n, slab - k, 0:rows]
            by = fields[s, 3 + n, slab] + c12 * (fields[s, 0, slab + k] + fields[s, 0, slab - k])
            gy = (yroll(by, -k) - yroll(by, k))[0:rows]
            gz = fields[s, 5 + n, slab, 0:rows] + (fields[s, 7 + n, slab + k, 0:rows] + fields[s, 7 + n, slab - k, 0:rows])
            out.append((gx, gy, gz))
    result = []
    for s in range(2):
        minus = -fields[s, 0, slab, 0:rows]
        result.append([minus * (near[1 - s][a] + far[s][a]) for a in range(3)])
    return result


def populations(s, rho, v, f, old=None):
    w = 1.0 / 36.0
    rt = (w * TAU_INV[s]) * rho
    vv = v[0] * v[0] + v[1] * v[1] + v[2] * v[2]
    vf = v[0] * f[0] + v[1] * f[1] + v[2] * f[2]
    a0 = rt * (1.0 - 1.5 * vv) - (3.0 * SRC[s] * w) * vf
    b = [3.0 * (rt * v[a] + (SRC[s] * w) * f[a]) for a in range(3)]
    g = [4.5 * rt * v[a] + (9.0 * SRC[s] * w) * f[a] for a in range(3)]
    diag = [v[a] * g[a] for a in range(3)]
    off = {(a, c): v[a] * g[c] + v[c] * g[a] for a, c in ((0, 1), (0, 2), (1, 2))}
    if old is not None:
        part = 1.0 - TAU_INV[s]
        ro = (w * part) * rho
        uu = old[0] * old[0] + old[1] * old[1] + old[2] * old[2]
        a0 = a0 + ro * (1.0 - 1.5 * uu)
        h = [4.5 * ro * old[a] for a in range(3)]
        b = [b[a] + 3.0 * ro * old[a] for a in range(3)]
        diag = [diag[a] + old[a] * h[a] for a in range(3)]
        off = {(a, c): off[a, c] + 2.0 * (old[a] * h[c]) for a, c in off}
    post = {(0, 0, 0): 12.0 * a0}
    for a in range(3):
        even, odd = a0 + diag[a], b[a]
        unit = [0, 0, 0]
        unit[a] = 1
        post[tuple(unit)] = 2.0 * (even + odd)
        post[tuple(-q for q in unit)] = 2.0 * (even - odd)
    for a, c in off:
        base = a0 + (diag[a] + diag[c])
        for sign in (1, -1):
            even = base + off[a, c] if sign == 1 else base - off[a, c]
            odd = b[a] + b[c] if sign == 1 else b[a] - b[c]
            unit = [0, 0, 0]
            unit[a], unit[c] = 1, sign
            post[tuple(unit)] = even + odd
            post[tuple(-q for q in unit)] = even - odd
    return post


def compute_kernel(ro, uo, zp, rx, ux, ry, uy, re, ue, zf, ze, out_ref,
                   rho, vel, zr, fld, pops, qs, qz, rho1, mom, sout, outx, sem):
    for e in range(20):
        dx, x = (0, e + 2) if e < 6 else (1, e - 6) if e < 14 else (2, e - 14)
        for c in range(2):
            for j in range(4):
                if dx == 1:
                    r0 = 6 * x
                    part = (ry[0, c, r0:r0 + 6] if j == 0 else ry[1, c, r0:r0 + 6] if j == 3 else
                            ro[c, j - 1, r0:r0 + 6])
                else:
                    sx = dx // 2
                    r0 = 6 * x - (8 if sx == 0 else 0)
                    part = (re[sx, 0, c, r0:r0 + 6] if j == 0 else re[sx, 1, c, r0:r0 + 6] if j == 3 else
                            rx[sx, c, j - 1, r0:r0 + 6])
                rho[c, e, 6 * j:6 * j + 6, :] = part
    for k in range(16):
        dx, x = (0, k + 4) if k < 4 else (1, k - 4) if k < 12 else (2, k - 12)
        for f in range(3):
            for j in range(5):
                if dx == 1:
                    r0 = 4 * x
                    part = (uy[0, f, r0:r0 + 4] if j == 0 else uy[1, f, r0:r0 + 4] if j == 4 else
                            uo[f, j - 1, r0:r0 + 4])
                else:
                    sx = dx // 2
                    r0 = 4 * x - (16 if sx == 0 else 0)
                    part = (ue[sx, 0, f, r0:r0 + 4] if j == 0 else ue[sx, 1, f, r0:r0 + 4] if j == 4 else
                            ux[sx, f, j - 1, r0:r0 + 4])
                vel[f, k, 2 + 4 * j:6 + 4 * j, :] = part
    for zs in range(2):
        for dx in range(3):
            for k in range(2):
                zr[zs, dx, k, 0:6] = ze[zs, dx, 0, k, 0:6]
                zr[zs, dx, k, 6:12] = zf[zs, dx, 0, k, 0:6]
                zr[zs, dx, k, 12:18] = zf[zs, dx, 1, k, 0:6]
                zr[zs, dx, k, 18:24] = ze[zs, dx, 1, k, 0:6]
    lane = lane_of(24)
    in_seg = lane % 18
    for f in range(5):
        merged = []
        for zs in range(2):
            m = jnp.zeros((24, 128), F32)
            for dx, (e_lo, e_hi) in enumerate(((0, 6), (6, 14), (14, 20))):
                off = 6 + 8 * (dx - 1)
                for x_lo, x_hi in ((0, 4), (4, 8)) if f == 4 else ((0, 8),):
                    a, b = max(e_lo, x_lo + off), min(e_hi, x_hi + off)
                    if a >= b:
                        continue
                    tile, l0 = z_place(f, x_lo)
                    shift = 6 * (x_lo + off) - l0
                    m = jnp.where((lane >= 6 * a) & (lane < 6 * b), lroll(zr[zs, dx, tile], shift), m)
            merged.append(m)
        for xo in range(3):
            low = lroll(merged[0], -6 * xo)
            high = lroll(merged[1], 6 - 6 * xo)
            for seg in range(7):
                e = 3 * seg + xo
                if f < 2:
                    if e > 19:
                        continue
                    val = rho[f, e]
                else:
                    if e < 2 or e > 17:
                        continue
                    val = vel[f - 2, e - 2]
                val = lroll(val, 18 * seg + 6)
                low = jnp.where((lane >= 18 * seg + 6) & (lane < 18 * seg + 18), val, low)
                start = (18 * seg - 6) % 128
                if seg == 0:
                    high = jnp.where((lane >= 122) | (lane < 6), val, high)
                else:
                    high = jnp.where((lane >= start) & (lane < start + 12), val, high)
            if f < 2:
                for base, v in ((20, low), (27, high)):
                    rho[f, base + 2 + xo] = v
                    if xo == 0:
                        rho[f, base + 5] = lroll(v, -18)
                    if xo == 1:
                        rho[f, base] = lroll(v, 18)
                        rho[f, base + 6] = lroll(v, -18)
                    if xo == 2:
                        rho[f, base + 1] = lroll(v, 18)
            else:
                vel[f - 2, 16 + xo] = low
                vel[f - 2, 19 + xo] = high

    @pl.loop(0, NS1)
    def _(slab):
        stage_a(rho, slab, None, fld)

    @pl.loop(0, 22)
    def _(j):
        late, later = (j >= 16).astype(jnp.int32), (j >= 19).astype(jnp.int32)
        slab = j + 2 + 4 * late + 4 * later
        dst = j + late + 2 * later
        fs = force(fld, slab, 24)
        r = [rho[s, slab] for s in range(2)]
        u = [vel[a, j] for a in range(3)]
        half = 0.5 / (r[0] + r[1])
        v = [u[a] + half * (fs[0][a] + fs[1][a]) for a in range(3)]
        zsum = {}
        for s in range(2):
            post = populations(s, r[s], v, fs[s], u if s == 1 else None)
            sums = {}
            for i, (cx, cy, cz) in enumerate(VELS):
                val = lroll(post[VELS[i]], cz)
                if s == 1:
                    pops[i, dst, 8:32] = val
                sums[cx, cy] = val if (cx, cy) not in sums else sums[cx, cy] + val
                if cz:
                    part = val if cz == 1 else -val
                    zsum[cx, cy] = part if (cx, cy) not in zsum else zsum[cx, cy] + part
            for n, key in enumerate(GROUPS):
                qs[s, n, dst, 8:32] = sums[key]
        for n, key in enumerate(ZGROUPS):
            qz[n, dst, 8:32] = zsum[key]

    for base in (16, 21):
        for n, (cx, cy) in enumerate(GROUPS):
            for s in range(2):
                if cx == 1:
                    qs[s, n, base, 8:32] = lroll(qs[s, n, base + 3, 8:32], 18)
                if cx == -1:
                    qs[s, n, base + 4, 8:32] = lroll(qs[s, n, base + 1, 8:32], -18)
        for n, (cx, cy) in enumerate(ZGROUPS):
            if cx == 1:
                qz[n, base, 8:32] = lroll(qz[n, base + 3, 8:32], 18)
            if cx == -1:
                qz[n, base + 4, 8:32] = lroll(qz[n, base + 1, 8:32], -18)
        for i, (cx, cy, cz) in enumerate(VELS):
            if cx == 1:
                pops[i, base, 8:32] = lroll(pops[i, base + 3, 8:32], 18)
            if cx == -1:
                pops[i, base + 4, 8:32] = lroll(pops[i, base + 1, 8:32], -18)

    @pl.loop(0, 20)
    def _(g):
        late, later = (g >= 14).astype(jnp.int32), (g >= 17).astype(jnp.int32)
        src = g + 1 + 2 * late + 2 * later
        dst = g + 2 * late + 4 * later
        mx = my = 0.0
        for s in range(2):
            top = bottom = 0.0
            for n, (cx, cy) in enumerate(GROUPS):
                a = qs[s, n, src - cx, 13 - cy:29 - cy]
                top = top + a
                bottom = bottom + qs[s, n, src - cx, 5 - cy:13 - cy]
                mx = mx + cx * a if cx else mx
                my = my + cy * a if cy else my
            rho1[s, dst, 0:16] = top
            rho1[s, dst, 16:24] = bottom
        mz = 0.0
        for n, (cx, cy) in enumerate(ZGROUPS):
            mz = mz + qz[n, src - cx, 13 - cy:29 - cy]
        mom[0, dst], mom[1, dst], mom[2, dst] = mx, my, mz

    for base in (14, 21):
        for s in range(2):
            rho1[s, base] = lroll(rho1[s, base + 3], 18)
            rho1[s, base + 1] = lroll(rho1[s, base + 4], 18)
            rho1[s, base + 5] = lroll(rho1[s, base + 2], -18)
            rho1[s, base + 6] = lroll(rho1[s, base + 3], -18)

    @pl.loop(0, NS2)
    def _(slab):
        stage_a(rho1, slab, None, fld)

    def second(slab, src, write):
        fs = force(fld, slab, 16)
        r = [rho1[s, slab, 0:16] for s in range(2)]
        inv = 1.0 / (r[0] + r[1])
        v = [(mom[a, slab] + 0.5 * (fs[0][a] + fs[1][a])) * inv for a in range(3)]
        for s in range(2):
            post = populations(s, r[s], v, fs[s])
            for i, (cx, cy, cz) in enumerate(VELS):
                val = post[VELS[i]]
                if s == 1:
                    val = val - 0.25 * pops[i, src - cx, 13 - cy:29 - cy]
                write(s, i, yroll(lroll(val, cz), cy - 1))

    @pl.loop(0, 6)
    def _(t):
        later = (t >= 3).astype(jnp.int32)

        def write(s, i, val):
            sout[s, i, t] = val

        second(16 + t + 4 * later, 17 + t + 2 * later, write)

    lane16 = lane_of(16)
    seg16 = lane16 % 18
    from_low = (seg16 >= 6) & (seg16 < 12)
    edge = (lane16 < 6) | (lane16 >= 122)

    @pl.loop(0, 10)
    def _(k):
        e = k + 5
        seg = e // 3
        xo = e - 3 * seg
        shift = lax.rem(256 - 18 * seg - 6, 128)

        def write(s, i, val):
            cx = VELS[i][0]
            strip = jnp.where(from_low, sout[s, i, xo], sout[s, i, xo + 3])
            val = jnp.where(edge, pltpu.roll(strip, shift, 1), val)
            x = k - 1 + cx
            inside = (x >= 0) & (x < 8)
            outx[s, i, pl.ds(jnp.where(inside, x, 96), 12, stride=8)] = val[0:12]

        second(k + 2, k + 3, write)

    copy = pltpu.make_async_copy(outx.at[:, :, 0:96], out_ref, sem.at[0])
    copy.start()
    copy.wait()


def compute(parts):
    vmem = pl.BlockSpec(memory_space=pltpu.VMEM)
    return pl.pallas_call(
        compute_kernel,
        out_shape=jax.ShapeDtypeStruct((2, 19, 96, 128), F32),
        in_specs=[vmem] * len(parts),
        out_specs=pl.BlockSpec(memory_space=pltpu.HBM),
        scratch_shapes=[
            pltpu.VMEM((2, NS1, 24, 128), F32), pltpu.VMEM((3, 22, 24, 128), F32), pltpu.VMEM((2, 3, 2, 24, 128), F32),
            pltpu.VMEM((2, 9, NS1, 24, 128), F32), pltpu.VMEM((19, NP1, 40, 128), F32),
            pltpu.VMEM((2, 9, NP1, 40, 128), F32), pltpu.VMEM((5, NP1, 40, 128), F32),
            pltpu.VMEM((2, NS2, 24, 128), F32), pltpu.VMEM((3, NS2, 16, 128), F32),
            pltpu.VMEM((2, 19, 6, 16, 128), F32),
            pltpu.VMEM((2, 19, 192, 128), F32), pltpu.SemaphoreType.DMA((1,))],
        compiler_params=pltpu.CompilerParams(vmem_limit_bytes=40 << 20),
    )(*parts)


def local(labels, density_jitter, velocity):
    rows = [jnp.swapaxes(a, -3, -2).reshape(a.shape[:-3] + (96, 128)) for a in (labels, density_jitter, velocity)]
    out = compute(exchange(*rows))
    return jnp.swapaxes(out.reshape(2, 19, 12, 8, 128), 2, 3)


def solution(mesh):
    in_specs = (P("gx", "gy", "gz"), P(None, "gx", "gy", "gz"), P(None, "gx", "gy", "gz"))
    out_specs = P(None, None, "gx", "gy", "gz")
    return jax.shard_map(local, mesh=mesh, in_specs=in_specs, out_specs=out_specs, check_vma=False)
```

```python
import functools
import itertools

import jax
import jax.numpy as jnp
from jax import lax
from jax.experimental import pallas as pl
from jax.experimental.pallas import tpu as pltpu
from jax.sharding import PartitionSpec as P

MESH = pl.DeviceIdType.MESH
F32 = jnp.float32
VELS = [(0, 0, 0), (1, 0, 0), (-1, 0, 0), (0, 1, 0), (0, -1, 0), (0, 0, 1), (0, 0, -1),
        (1, 1, 0), (-1, -1, 0), (1, -1, 0), (-1, 1, 0), (1, 0, 1), (-1, 0, -1),
        (1, 0, -1), (-1, 0, 1), (0, 1, 1), (0, -1, -1), (0, 1, -1), (0, -1, 1)]
TAU_INV = (1.0, 1.25)
SRC = (0.5, 0.375)
REACHES = ((1, 0.25, 0.125), (2, 0.5 / 6, 0.5 / 12))
GROUPS = [(a, b) for a in (-1, 0, 1) for b in (-1, 0, 1)]
ZGROUPS = [(0, 0), (1, 0), (-1, 0), (0, 1), (0, -1)]
NEIGHBOURS = [d for d in itertools.product((-1, 0, 1), repeat=3) if d != (0, 0, 0)]
OWN = [(2, 2, 48, 128), (3, 3, 32, 128)]
Z_PACK = (2, 2, 2, 8, 128)
EXCHANGED = OWN + [
    (2, 2, 2, 40, 128), (2, 3, 3, 16, 128),
             (2, 2, 48, 128), (2, 3, 32, 128),
             (2, 2, 2, 40, 128), (2, 2, 3, 16, 128),
             (2, 3, 2, 2, 8, 128), (2, 3, 2, 2, 8, 128)]


def lane_of(rows):
    return lax.broadcasted_iota(jnp.int32, (rows, 128), 1)


def lroll(v, k):
    k = k % 128
    return v if isinstance(k, int) and k == 0 else pltpu.roll(v, k, 1)


def yroll(v, k):
    k = k % v.shape[0]
    return v if k == 0 else pltpu.roll(v, k, 0)


def z_place(f, x):
    if f < 2:
        return 0, 48 * f + 6 * x
    if f < 4:
        return 1, 48 * (f - 2) + 6 * x
    return (0, 96 + 6 * x) if x < 4 else (1, 96 + 6 * (x - 4))


def exchange_kernel(lab_ref, jit_ref, vel_ref, ro_out, uo_out, rx, ux, ry, uy, re, ue, zf, ze,
                    lab, rho, vel, ro, uo, zp, load_sem, store_sem, ssem, rsem, answer):
    ix, iy, iz = lax.axis_index("gx"), lax.axis_index("gy"), lax.axis_index("gz")
    nx, ny, nz = lax.axis_size("gx"), lax.axis_size("gy"), lax.axis_size("gz")

    def device(d):
        return (lax.rem(ix + d[0] + nx, nx), lax.rem(iy + d[1] + ny, ny), lax.rem(iz + d[2] + nz, nz))

    place = lax.rem(iz, 8)
    first_up, first_down = place != 7, place == 0
    barrier = pltpu.get_barrier_semaphore()

    def tell(semaphore, dz):
        for d in NEIGHBOURS:
            if d[2] == dz:
                pl.semaphore_signal(semaphore, inc=1, device_id=device(d), device_id_type=MESH)

    tell(barrier, 0)
    pl.when(first_up)(lambda: tell(barrier, 1))
    pl.when(first_down)(lambda: tell(barrier, -1))
    loads = [pltpu.make_async_copy(a, b, load_sem.at[n])
             for n, (a, b) in enumerate(((lab_ref, lab), (jit_ref, rho), (vel_ref, vel)))]
    for load in loads:
        load.start()
    for load in loads:
        load.wait()
    rho[0] = jnp.where(lab[...] == 1, 2.0, 0.15).astype(F32) * rho[0]
    rho[1] = jnp.where(lab[...] == 1, 0.15, 2.0).astype(F32) * rho[1]
    lane = lane_of(6)
    for h in range(2):
        packs = [[jnp.zeros((6, 128), F32) for _ in range(2)] for _ in range(2)]
        for f in range(5):
            for x in range(8):
                rows = pl.ds(48 * h + x, 6, stride=8)
                val = rho[f, rows, :] if f < 2 else vel[f - 2, rows, :]
                if f < 2:
                    ro[f, h, 6 * x:6 * x + 6, :] = val
                k, l0 = z_place(f, x)
                here = (lane >= l0) & (lane < l0 + 6)
                packs[0][k] = jnp.where(here, lroll(val, l0), packs[0][k])
                packs[1][k] = jnp.where(here, lroll(val, l0 + 6), packs[1][k])
        for zs in range(2):
            for k in range(2):
                zp[zs, h, k, 0:6, :] = packs[zs][k]
                zp[zs, h, k, 6:8, :] = packs[zs][k][0:2]
    for f in range(3):
        for g in range(3):
            for x in range(8):
                uo[f, g, 4 * x:4 * x + 4, :] = vel[f, pl.ds(32 * g + x, 4, stride=8), :]
    pl.semaphore_wait(barrier, 8 + 9 * (place == 7).astype(jnp.int32) + 9 * (place != 0).astype(jnp.int32))
    pl.when(jnp.logical_not(first_up))(lambda: tell(answer.at[1], 1))
    pl.when(jnp.logical_not(first_down))(lambda: tell(answer.at[0], -1))

    stores = [pltpu.make_async_copy(a, b, store_sem.at[n])
              for n, (a, b) in enumerate(((ro, ro_out), (uo, uo_out)))]
    copies = []

    def plan(src, dst, d):
        n = len(copies)
        copy = pltpu.make_async_remote_copy(src_ref=src, dst_ref=dst, send_sem=ssem.at[n], recv_sem=rsem.at[n],
                                            device_id=device(d), device_id_type=MESH)
        copies.append(copy)
        return copy

    def send(src, dst, d):
        plan(src, dst, d).start()

    def plan_z(dz):
        zs_mine, zs_theirs = (1, 0) if dz == 1 else (0, 1)
        group = []
        for dx in (0, 1, -1):
            group.append(plan(zp.at[zs_mine], zf.at[zs_theirs, 1 - dx], (dx, 0, dz)))
            for dy in (1, -1):
                h, side = (1, 0) if dy == 1 else (0, 1)
                group.append(plan(zp.at[zs_mine, h], ze.at[zs_theirs, 1 - dx, side], (dx, dy, dz)))
        return group

    up, down = plan_z(1), plan_z(-1)

    def start(group):
        for copy in group:
            copy.start()

    pl.when(jnp.logical_not(first_up))(lambda: start(up))
    pl.when(jnp.logical_not(first_down))(lambda: start(down))
    for dx in (1, -1):
        sx, r0, u0 = (0, 8, 16) if dx == 1 else (1, 0, 0)
        send(ro.at[:, :, r0:r0 + 40], rx.at[sx], (dx, 0, 0))
        send(uo.at[:, :, u0:u0 + 16], ux.at[sx], (dx, 0, 0))
        for dy in (1, -1):
            sy, h, g = (0, 1, 2) if dy == 1 else (1, 0, 0)
            send(ro.at[:, h, r0:r0 + 40], re.at[sx, sy], (dx, dy, 0))
            send(uo.at[:, g, u0:u0 + 16], ue.at[sx, sy], (dx, dy, 0))
    for dy in (1, -1):
        sy, h, g = (0, 1, 2) if dy == 1 else (1, 0, 0)
        send(ro.at[:, h], ry.at[sy], (0, dy, 0))
        send(uo.at[:, g], uy.at[sy], (0, dy, 0))

    for store in stores:
        store.start()

    @pl.when(first_down)
    def _():
        pl.semaphore_wait(answer.at[1], 9)
        start(down)

    @pl.when(first_up)
    def _():
        pl.semaphore_wait(answer.at[0], 9)
        start(up)

    for copy in copies + stores:
        copy.wait()


def exchange(labels, jitter, velocity):
    anywhere = pl.BlockSpec(memory_space=pl.ANY)
    return pl.pallas_call(
        exchange_kernel,
        out_shape=[jax.ShapeDtypeStruct(s, F32) for s in EXCHANGED],
        in_specs=[anywhere] * 3,
        out_specs=[anywhere] * len(EXCHANGED),
        scratch_shapes=[pltpu.VMEM((96, 128), jnp.int32), pltpu.VMEM((2, 96, 128), F32), pltpu.VMEM((3, 96, 128), F32)]
        + [pltpu.VMEM(s, F32) for s in OWN + [Z_PACK]]
        + [pltpu.SemaphoreType.DMA((3,)), pltpu.SemaphoreType.DMA((2,)), pltpu.SemaphoreType.DMA((34,)),
           pltpu.SemaphoreType.DMA((34,)), pltpu.SemaphoreType.REGULAR((2,))],
        compiler_params=pltpu.CompilerParams(collective_id=0, has_side_effects=True, vmem_limit_bytes=60 << 20),
    )(labels, jitter, velocity)


NS1, NP1, NS2 = 34, 26, 28


def stage_z(src, slab, fp, fz, p0):
    for s in range(2):
        p = 1.0 - jnp.exp(-src[s, slab])
        fp[s, slab, p0:p0 + 24] = p
        for n, (k, c6, c12) in enumerate(REACHES):
            up, down = lroll(p, -k), lroll(p, k)
            fz[s, n, 0, slab, p0:p0 + 24] = c6 * p + c12 * (up + down)
            fz[s, n, 1, slab, p0:p0 + 24] = c12 * (up - down)


def stage_y(slab, fp, fz, fy, rows):
    for s in range(2):
        for n, (k, c6, c12) in enumerate(REACHES):
            p_up, p_down = fp[s, slab, 8 + k:8 + k + rows], fp[s, slab, 8 - k:8 - k + rows]
            b_up, b_down = fz[s, n, 0, slab, 8 + k:8 + k + rows], fz[s, n, 0, slab, 8 - k:8 - k + rows]
            d_up, d_down = fz[s, n, 1, slab, 8 + k:8 + k + rows], fz[s, n, 1, slab, 8 - k:8 - k + rows]
            fy[s, n, 0, slab, 0:rows] = fz[s, n, 0, slab, 8:8 + rows] + c12 * (p_up + p_down)
            fy[s, n, 1, slab, 0:rows] = b_up - b_down
            fy[s, n, 2, slab, 0:rows] = c12 * (p_up - p_down)
            fy[s, n, 3, slab, 0:rows] = 2.0 * fz[s, n, 1, slab, 8:8 + rows] + (d_up + d_down)


def force(fp, fz, fy, slab, rows):
    near, far = [], []
    for s in range(2):
        for n, out in enumerate((near, far)):
            k = n + 1
            gx = fy[s, n, 0, slab + k, 0:rows] - fy[s, n, 0, slab - k, 0:rows]
            gy = fy[s, n, 1, slab, 0:rows] + (fy[s, n, 2, slab + k, 0:rows] + fy[s, n, 2, slab - k, 0:rows])
            gz = fy[s, n, 3, slab, 0:rows] + (fz[s, n, 1, slab + k, 8:8 + rows] + fz[s, n, 1, slab - k, 8:8 + rows])
            out.append((gx, gy, gz))
    result = []
    for s in range(2):
        minus = -fp[s, slab, 8:8 + rows]
        result.append([minus * (near[1 - s][a] + far[s][a]) for a in range(3)])
    return result


def populations(s, rho, v, f, old=None):
    w = 1.0 / 36.0
    rt = (w * TAU_INV[s]) * rho
    vv = v[0] * v[0] + v[1] * v[1] + v[2] * v[2]
    vf = v[0] * f[0] + v[1] * f[1] + v[2] * f[2]
    a0 = rt * (1.0 - 1.5 * vv) - (3.0 * SRC[s] * w) * vf
    b = [3.0 * (rt * v[a] + (SRC[s] * w) * f[a]) for a in range(3)]
    g = [4.5 * rt * v[a] + (9.0 * SRC[s] * w) * f[a] for a in range(3)]
    diag = [v[a] * g[a] for a in range(3)]
    off = {(a, c): v[a] * g[c] + v[c] * g[a] for a, c in ((0, 1), (0, 2), (1, 2))}
    if old is not None:
        part = 1.0 - TAU_INV[s]
        ro = (w * part) * rho
        uu = old[0] * old[0] + old[1] * old[1] + old[2] * old[2]
        a0 = a0 + ro * (1.0 - 1.5 * uu)
        h = [4.5 * ro * old[a] for a in range(3)]
        b = [b[a] + 3.0 * ro * old[a] for a in range(3)]
        diag = [diag[a] + old[a] * h[a] for a in range(3)]
        off = {(a, c): off[a, c] + 2.0 * (old[a] * h[c]) for a, c in off}
    post = {(0, 0, 0): 12.0 * a0}
    for a in range(3):
        even, odd = a0 + diag[a], b[a]
        unit = [0, 0, 0]
        unit[a] = 1
        post[tuple(unit)] = 2.0 * (even + odd)
        post[tuple(-q for q in unit)] = 2.0 * (even - odd)
    for a, c in off:
        base = a0 + (diag[a] + diag[c])
        for sign in (1, -1):
            even = base + off[a, c] if sign == 1 else base - off[a, c]
            odd = b[a] + b[c] if sign == 1 else b[a] - b[c]
            unit = [0, 0, 0]
            unit[a], unit[c] = 1, sign
            post[tuple(unit)] = even + odd
            post[tuple(-q for q in unit)] = even - odd
    return post


def compute_kernel(*refs):
    parts, out_ref, held, load_sem = refs[:10], refs[10], refs[11:21], refs[21]
    loads = [pltpu.make_async_copy(a, b, load_sem.at[n]) for n, (a, b) in enumerate(zip(parts, held))]
    for load in loads:
        load.start()
    for load in loads:
        load.wait()
    compute_parts(*held, out_ref, *refs[22:])


def compute_parts(ro, uo, rx, ux, ry, uy, re, ue, zf, ze, out_ref,
                  rho, vel, zr, fp, fz, fy, pops, qs, qz, rho1, mom, kept, sout, outx, sem):
    for e in range(20):
        dx, x = (0, e + 2) if e < 6 else (1, e - 6) if e < 14 else (2, e - 14)
        for c in range(2):
            for j in range(4):
                if dx == 1:
                    r0 = 6 * x
                    part = (ry[0, c, r0:r0 + 6] if j == 0 else ry[1, c, r0:r0 + 6] if j == 3 else
                            ro[c, j - 1, r0:r0 + 6])
                else:
                    sx = dx // 2
                    r0 = 6 * x - (8 if sx == 0 else 0)
                    part = (re[sx, 0, c, r0:r0 + 6] if j == 0 else re[sx, 1, c, r0:r0 + 6] if j == 3 else
                            rx[sx, c, j - 1, r0:r0 + 6])
                rho[c, e, 6 * j:6 * j + 6, :] = part
    for k in range(16):
        dx, x = (0, k + 4) if k < 4 else (1, k - 4) if k < 12 else (2, k - 12)
        for f in range(3):
            for j in range(5):
                if dx == 1:
                    r0 = 4 * x
                    part = (uy[0, f, r0:r0 + 4] if j == 0 else uy[1, f, r0:r0 + 4] if j == 4 else
                            uo[f, j - 1, r0:r0 + 4])
                else:
                    sx = dx // 2
                    r0 = 4 * x - (16 if sx == 0 else 0)
                    part = (ue[sx, 0, f, r0:r0 + 4] if j == 0 else ue[sx, 1, f, r0:r0 + 4] if j == 4 else
                            ux[sx, f, j - 1, r0:r0 + 4])
                vel[f, k, 2 + 4 * j:6 + 4 * j, :] = part
    for zs in range(2):
        for dx in range(3):
            for k in range(2):
                zr[zs, dx, k, 0:6] = ze[zs, dx, 0, k, 0:6]
                zr[zs, dx, k, 6:12] = zf[zs, dx, 0, k, 0:6]
                zr[zs, dx, k, 12:18] = zf[zs, dx, 1, k, 0:6]
                zr[zs, dx, k, 18:24] = ze[zs, dx, 1, k, 0:6]
    lane = lane_of(24)
    in_seg = lane % 18
    for f in range(5):
        merged = []
        for zs in range(2):
            m = jnp.zeros((24, 128), F32)
            for dx, (e_lo, e_hi) in enumerate(((0, 6), (6, 14), (14, 20))):
                off = 6 + 8 * (dx - 1)
                for x_lo, x_hi in ((0, 4), (4, 8)) if f == 4 else ((0, 8),):
                    a, b = max(e_lo, x_lo + off), min(e_hi, x_hi + off)
                    if a >= b:
                        continue
                    tile, l0 = z_place(f, x_lo)
                    shift = 6 * (x_lo + off) - l0
                    m = jnp.where((lane >= 6 * a) & (lane < 6 * b), lroll(zr[zs, dx, tile], shift), m)
            merged.append(m)
        for xo in range(3):
            low = lroll(merged[0], -6 * xo)
            high = lroll(merged[1], 6 - 6 * xo)
            for seg in range(7):
                e = 3 * seg + xo
                if f < 2:
                    if e > 19:
                        continue
                    val = rho[f, e]
                else:
                    if e < 2 or e > 17:
                        continue
                    val = vel[f - 2, e - 2]
                val = lroll(val, 18 * seg + 6)
                low = jnp.where((lane >= 18 * seg + 6) & (lane < 18 * seg + 18), val, low)
                start = (18 * seg - 6) % 128
                if seg == 0:
                    high = jnp.where((lane >= 122) | (lane < 6), val, high)
                else:
                    high = jnp.where((lane >= start) & (lane < start + 12), val, high)
            if f < 2:
                for base, v in ((20, low), (27, high)):
                    rho[f, base + 2 + xo] = v
                    if xo == 0:
                        rho[f, base + 5] = lroll(v, -18)
                    if xo == 1:
                        rho[f, base] = lroll(v, 18)
                        rho[f, base + 6] = lroll(v, -18)
                    if xo == 2:
                        rho[f, base + 1] = lroll(v, 18)
            else:
                vel[f - 2, 16 + xo] = low
                vel[f - 2, 19 + xo] = high

    @pl.loop(0, NS1, unroll=17)
    def _(slab):
        stage_z(rho, slab, fp, fz, 8)

    @pl.loop(0, NS1, unroll=17)
    def _(slab):
        stage_y(slab, fp, fz, fy, 24)

    @pl.loop(0, 22, unroll=2)
    def _(j):
        late, later = (j >= 16).astype(jnp.int32), (j >= 19).astype(jnp.int32)
        slab = j + 2 + 4 * late + 4 * later
        dst = j + late + 2 * later
        fs = force(fp, fz, fy, slab, 24)
        r = [rho[s, slab] for s in range(2)]
        u = [vel[a, j] for a in range(3)]
        half = 0.5 / (r[0] + r[1])
        v = [u[a] + half * (fs[0][a] + fs[1][a]) for a in range(3)]
        zsum = {}
        for s in range(2):
            post = populations(s, r[s], v, fs[s], u if s == 1 else None)
            sums = {}
            for i, (cx, cy, cz) in enumerate(VELS):
                val = lroll(post[VELS[i]], cz)
                if s == 1:
                    pops[i, dst, 8:32] = val
                sums[cx, cy] = val if (cx, cy) not in sums else sums[cx, cy] + val
                if cz:
                    part = val if cz == 1 else -val
                    zsum[cx, cy] = part if (cx, cy) not in zsum else zsum[cx, cy] + part
            for n, key in enumerate(GROUPS):
                qs[s, n, dst, 8:32] = sums[key]
        for n, key in enumerate(ZGROUPS):
            qz[n, dst, 8:32] = zsum[key]

    for base in (16, 21):
        for n, (cx, cy) in enumerate(GROUPS):
            for s in range(2):
                if cx == 1:
                    qs[s, n, base, 8:32] = lroll(qs[s, n, base + 3, 8:32], 18)
                if cx == -1:
                    qs[s, n, base + 4, 8:32] = lroll(qs[s, n, base + 1, 8:32], -18)
        for n, (cx, cy) in enumerate(ZGROUPS):
            if cx == 1:
                qz[n, base, 8:32] = lroll(qz[n, base + 3, 8:32], 18)
            if cx == -1:
                qz[n, base + 4, 8:32] = lroll(qz[n, base + 1, 8:32], -18)
        for i, (cx, cy, cz) in enumerate(VELS):
            if cx == 1:
                pops[i, base, 8:32] = lroll(pops[i, base + 3, 8:32], 18)
            if cx == -1:
                pops[i, base + 4, 8:32] = lroll(pops[i, base + 1, 8:32], -18)

    @pl.loop(0, 20, unroll=4)
    def _(g):
        late, later = (g >= 14).astype(jnp.int32), (g >= 17).astype(jnp.int32)
        src = g + 1 + 2 * late + 2 * later
        dst = g + 2 * late + 4 * later
        mx = my = 0.0
        for s in range(2):
            top = bottom = 0.0
            for n, (cx, cy) in enumerate(GROUPS):
                a = qs[s, n, src - cx, 13 - cy:29 - cy]
                top = top + a
                bottom = bottom + qs[s, n, src - cx, 5 - cy:13 - cy]
                mx = mx + cx * a if cx else mx
                my = my + cy * a if cy else my
            rho1[s, dst, 8:24] = top
            rho1[s, dst, 0:8] = bottom
        mz = 0.0
        for n, (cx, cy) in enumerate(ZGROUPS):
            mz = mz + qz[n, src - cx, 13 - cy:29 - cy]
        mom[0, dst], mom[1, dst], mom[2, dst] = mx, my, mz

    for base in (14, 21):
        for s in range(2):
            rho1[s, base] = lroll(rho1[s, base + 3], 18)
            rho1[s, base + 1] = lroll(rho1[s, base + 4], 18)
            rho1[s, base + 5] = lroll(rho1[s, base + 2], -18)
            rho1[s, base + 6] = lroll(rho1[s, base + 3], -18)

    @pl.loop(0, NS2, unroll=14)
    def _(slab):
        stage_z(rho1, slab, fp, fz, 0)

    @pl.loop(0, NS2, unroll=14)
    def _(slab):
        stage_y(slab, fp, fz, fy, 16)

    def motion(slab):
        fs = force(fp, fz, fy, slab, 16)
        inv = 1.0 / (rho1[0, slab, 8:24] + rho1[1, slab, 8:24])
        return [(mom[a, slab] + 0.5 * (fs[0][a] + fs[1][a])) * inv for a in range(3)], fs

    def second(s, slab, src, v, f, write):
        post = populations(s, rho1[s, slab, 8:24], v, f)
        for i, (cx, cy, cz) in enumerate(VELS):
            val = post[VELS[i]]
            if s == 1:
                val = val - 0.25 * pops[i, src - cx, 13 - cy:29 - cy]
            write(i, yroll(lroll(val, cz), cy - 1))

    @pl.loop(0, 6, unroll=2)
    def _(t):
        later = (t >= 3).astype(jnp.int32)

        v, fs = motion(16 + t + 4 * later)
        for s in range(2):
            def write(i, val):
                sout[s, i, t] = val

            second(s, 16 + t + 4 * later, 17 + t + 2 * later, v, fs[s], write)

    lane16 = lane_of(16)
    seg16 = lane16 % 18
    from_low = (seg16 >= 6) & (seg16 < 12)
    edge = (lane16 < 6) | (lane16 >= 122)

    def finish(s, k, v, f):
        e = k + 5
        seg = e // 3
        xo = e - 3 * seg
        shift = lax.rem(256 - 18 * seg - 6, 128)

        def write(i, val):
            strip = jnp.where(from_low, sout[s, i, xo], sout[s, i, xo + 3])
            val = jnp.where(edge, pltpu.roll(strip, shift, 1), val)
            x = k - 1 + VELS[i][0]
            outx[s, i, pl.ds(jnp.where((x >= 0) & (x < 8), x, 96), 12, stride=8)] = val[0:12]

        second(s, k + 2, k + 3, v, f, write)

    @pl.loop(0, 10, unroll=2)
    def _(k):
        v, fs = motion(k + 2)
        for a in range(3):
            kept[a, k] = v[a]
            kept[3 + a, k] = fs[1][a]
        finish(0, k, v, fs[0])

    first = pltpu.make_async_copy(outx.at[0, :, 0:96], out_ref.at[0], sem.at[0])
    first.start()

    @pl.loop(0, 10, unroll=2)
    def _(k):
        finish(1, k, [kept[a, k] for a in range(3)], [kept[3 + a, k] for a in range(3)])

    second_half = pltpu.make_async_copy(outx.at[1, :, 0:96], out_ref.at[1], sem.at[1])
    second_half.start()
    first.wait()
    second_half.wait()


def compute(parts):
    anywhere = pl.BlockSpec(memory_space=pl.ANY)
    return pl.pallas_call(
        compute_kernel,
        out_shape=jax.ShapeDtypeStruct((2, 19, 96, 128), F32),
        in_specs=[anywhere] * len(parts),
        out_specs=anywhere,
        scratch_shapes=[pltpu.VMEM(part.shape, F32) for part in parts] + [
            pltpu.SemaphoreType.DMA((len(parts),)), pltpu.VMEM((2, NS1, 24, 128), F32), pltpu.VMEM((3, 22, 24, 128), F32), pltpu.VMEM((2, 3, 2, 24, 128), F32),
            pltpu.VMEM((2, NS1, 40, 128), F32), pltpu.VMEM((2, 2, 2, NS1, 40, 128), F32),
            pltpu.VMEM((2, 2, 4, NS1, 24, 128), F32), pltpu.VMEM((19, NP1, 40, 128), F32),
            pltpu.VMEM((2, 9, NP1, 40, 128), F32), pltpu.VMEM((5, NP1, 40, 128), F32),
            pltpu.VMEM((2, NS2, 24, 128), F32), pltpu.VMEM((3, NS2, 16, 128), F32),
            pltpu.VMEM((6, 10, 16, 128), F32),
            pltpu.VMEM((2, 19, 6, 16, 128), F32),
            pltpu.VMEM((2, 19, 192, 128), F32), pltpu.SemaphoreType.DMA((2,))],
        compiler_params=pltpu.CompilerParams(vmem_limit_bytes=60 << 20),
    )(*parts)


def local(labels, density_jitter, velocity):
    rows = [jnp.swapaxes(a, -3, -2).reshape(a.shape[:-3] + (96, 128)) for a in (labels, density_jitter, velocity)]
    out = compute(exchange(*rows))
    return jnp.swapaxes(out.reshape(2, 19, 12, 8, 128), 2, 3)


def solution(mesh):
    in_specs = (P("gx", "gy", "gz"), P(None, "gx", "gy", "gz"), P(None, "gx", "gy", "gz"))
    out_specs = P(None, None, "gx", "gy", "gz")
    return jax.shard_map(local, mesh=mesh, in_specs=in_specs, out_specs=out_specs, check_vma=False)
```

```python
import functools
import itertools

import jax
import jax.numpy as jnp
from jax import lax
from jax.experimental import pallas as pl
from jax.experimental.pallas import tpu as pltpu
from jax.sharding import PartitionSpec as P

MESH = pl.DeviceIdType.MESH
F32 = jnp.float32
VELS = [(0, 0, 0), (1, 0, 0), (-1, 0, 0), (0, 1, 0), (0, -1, 0), (0, 0, 1), (0, 0, -1),
        (1, 1, 0), (-1, -1, 0), (1, -1, 0), (-1, 1, 0), (1, 0, 1), (-1, 0, -1),
        (1, 0, -1), (-1, 0, 1), (0, 1, 1), (0, -1, -1), (0, 1, -1), (0, -1, 1)]
TAU_INV = (1.0, 1.25)
SRC = (0.5, 0.375)
REACHES = ((1, 0.25, 0.125), (2, 0.5 / 6, 0.5 / 12))
GROUPS = [(a, b) for a in (-1, 0, 1) for b in (-1, 0, 1)]
ZGROUPS = [(0, 0), (1, 0), (-1, 0), (0, 1), (0, -1)]
NEIGHBOURS = [d for d in itertools.product((-1, 0, 1), repeat=3) if d != (0, 0, 0)]
OWN = [(2, 2, 48, 128), (3, 3, 32, 128)]
Z_PACK = (2, 2, 2, 8, 128)
EXCHANGED = OWN + [
    (2, 2, 2, 40, 128), (2, 3, 3, 16, 128),
             (2, 2, 48, 128), (2, 3, 32, 128),
             (2, 2, 2, 40, 128), (2, 2, 3, 16, 128),
             (2, 3, 2, 2, 8, 128), (2, 3, 2, 2, 8, 128)]


def lane_of(rows):
    return lax.broadcasted_iota(jnp.int32, (rows, 128), 1)


def lroll(v, k):
    k = k % 128
    return v if isinstance(k, int) and k == 0 else pltpu.roll(v, k, 1)


def yroll(v, k):
    k = k % v.shape[0]
    return v if k == 0 else pltpu.roll(v, k, 0)


def z_place(f, x):
    if f < 2:
        return 0, 48 * f + 6 * x
    if f < 4:
        return 1, 48 * (f - 2) + 6 * x
    return (0, 96 + 6 * x) if x < 4 else (1, 96 + 6 * (x - 4))


def exchange_kernel(lab_ref, jit_ref, vel_ref, ro_out, uo_out, rx, ux, ry, uy, re, ue, zf, ze,
                    lab, rho, vel, ro, uo, zp, load_sem, store_sem, ssem, rsem, answer):
    ix, iy, iz = lax.axis_index("gx"), lax.axis_index("gy"), lax.axis_index("gz")
    nx, ny, nz = lax.axis_size("gx"), lax.axis_size("gy"), lax.axis_size("gz")

    def device(d):
        return (lax.rem(ix + d[0] + nx, nx), lax.rem(iy + d[1] + ny, ny), lax.rem(iz + d[2] + nz, nz))

    place = lax.rem(iz, 8)
    first_up, first_down = place != 7, place == 0
    barrier = pltpu.get_barrier_semaphore()

    def tell(semaphore, dz):
        for d in NEIGHBOURS:
            if d[2] == dz:
                pl.semaphore_signal(semaphore, inc=1, device_id=device(d), device_id_type=MESH)

    tell(barrier, 0)
    pl.when(first_up)(lambda: tell(barrier, 1))
    pl.when(first_down)(lambda: tell(barrier, -1))
    loads = [pltpu.make_async_copy(a, b, load_sem.at[n])
             for n, (a, b) in enumerate(((lab_ref, lab), (jit_ref, rho), (vel_ref, vel)))]
    for load in loads:
        load.start()
    for load in loads:
        load.wait()
    rho[0] = jnp.where(lab[...] == 1, 2.0, 0.15).astype(F32) * rho[0]
    rho[1] = jnp.where(lab[...] == 1, 0.15, 2.0).astype(F32) * rho[1]
    lane = lane_of(6)
    for h in range(2):
        packs = [[jnp.zeros((6, 128), F32) for _ in range(2)] for _ in range(2)]
        for f in range(5):
            for x in range(8):
                rows = pl.ds(48 * h + x, 6, stride=8)
                val = rho[f, rows, :] if f < 2 else vel[f - 2, rows, :]
                if f < 2:
                    ro[f, h, 6 * x:6 * x + 6, :] = val
                k, l0 = z_place(f, x)
                here = (lane >= l0) & (lane < l0 + 6)
                packs[0][k] = jnp.where(here, lroll(val, l0), packs[0][k])
                packs[1][k] = jnp.where(here, lroll(val, l0 + 6), packs[1][k])
        for zs in range(2):
            for k in range(2):
                zp[zs, h, k, 0:6, :] = packs[zs][k]
                zp[zs, h, k, 6:8, :] = packs[zs][k][0:2]
    for f in range(3):
        for g in range(3):
            for x in range(8):
                uo[f, g, 4 * x:4 * x + 4, :] = vel[f, pl.ds(32 * g + x, 4, stride=8), :]
    pl.semaphore_wait(barrier, 8 + 9 * (place == 7).astype(jnp.int32) + 9 * (place != 0).astype(jnp.int32))
    pl.when(jnp.logical_not(first_up))(lambda: tell(answer.at[1], 1))
    pl.when(jnp.logical_not(first_down))(lambda: tell(answer.at[0], -1))

    stores = [pltpu.make_async_copy(a, b, store_sem.at[n])
              for n, (a, b) in enumerate(((ro, ro_out), (uo, uo_out)))]
    copies = []

    def plan(src, dst, d):
        n = len(copies)
        copy = pltpu.make_async_remote_copy(src_ref=src, dst_ref=dst, send_sem=ssem.at[n], recv_sem=rsem.at[n],
                                            device_id=device(d), device_id_type=MESH)
        copies.append(copy)
        return copy

    def send(src, dst, d):
        plan(src, dst, d).start()

    def plan_z(dz):
        zs_mine, zs_theirs = (1, 0) if dz == 1 else (0, 1)
        group = []
        for dx in (0, 1, -1):
            group.append(plan(zp.at[zs_mine], zf.at[zs_theirs, 1 - dx], (dx, 0, dz)))
            for dy in (1, -1):
                h, side = (1, 0) if dy == 1 else (0, 1)
                group.append(plan(zp.at[zs_mine, h], ze.at[zs_theirs, 1 - dx, side], (dx, dy, dz)))
        return group

    up, down = plan_z(1), plan_z(-1)

    def start(group):
        for copy in group:
            copy.start()

    pl.when(jnp.logical_not(first_up))(lambda: start(up))
    pl.when(jnp.logical_not(first_down))(lambda: start(down))
    for dx in (1, -1):
        sx, r0, u0 = (0, 8, 16) if dx == 1 else (1, 0, 0)
        send(ro.at[:, :, r0:r0 + 40], rx.at[sx], (dx, 0, 0))
        send(uo.at[:, :, u0:u0 + 16], ux.at[sx], (dx, 0, 0))
        for dy in (1, -1):
            sy, h, g = (0, 1, 2) if dy == 1 else (1, 0, 0)
            send(ro.at[:, h, r0:r0 + 40], re.at[sx, sy], (dx, dy, 0))
            send(uo.at[:, g, u0:u0 + 16], ue.at[sx, sy], (dx, dy, 0))
    for dy in (1, -1):
        sy, h, g = (0, 1, 2) if dy == 1 else (1, 0, 0)
        send(ro.at[:, h], ry.at[sy], (0, dy, 0))
        send(uo.at[:, g], uy.at[sy], (0, dy, 0))

    for store in stores:
        store.start()

    @pl.when(first_up)
    def _():
        pl.semaphore_wait(answer.at[0], 9)
        start(up)

    @pl.when(first_down)
    def _():
        pl.semaphore_wait(answer.at[1], 9)
        start(down)

    for copy in copies + stores:
        copy.wait()


def exchange(labels, jitter, velocity):
    anywhere = pl.BlockSpec(memory_space=pl.ANY)
    return pl.pallas_call(
        exchange_kernel,
        out_shape=[jax.ShapeDtypeStruct(s, F32) for s in EXCHANGED],
        in_specs=[anywhere] * 3,
        out_specs=[anywhere] * len(EXCHANGED),
        scratch_shapes=[pltpu.VMEM((96, 128), jnp.int32), pltpu.VMEM((2, 96, 128), F32), pltpu.VMEM((3, 96, 128), F32)]
        + [pltpu.VMEM(s, F32) for s in OWN + [Z_PACK]]
        + [pltpu.SemaphoreType.DMA((3,)), pltpu.SemaphoreType.DMA((2,)), pltpu.SemaphoreType.DMA((34,)),
           pltpu.SemaphoreType.DMA((34,)), pltpu.SemaphoreType.REGULAR((2,))],
        compiler_params=pltpu.CompilerParams(collective_id=0, has_side_effects=True, vmem_limit_bytes=60 << 20),
    )(labels, jitter, velocity)


NS1, NP1, NS2 = 34, 26, 28


def stage_z(src, slab, fp, fz, p0):
    for s in range(2):
        p = 1.0 - jnp.exp(-src[s, slab])
        fp[s, slab, p0:p0 + 24] = p
        for n, (k, c6, c12) in enumerate(REACHES):
            up, down = lroll(p, -k), lroll(p, k)
            fz[s, n, 0, slab, p0:p0 + 24] = c6 * p + c12 * (up + down)
            fz[s, n, 1, slab, p0:p0 + 24] = c12 * (up - down)


def stage_y(slab, fp, fz, fy, rows):
    for s in range(2):
        for n, (k, c6, c12) in enumerate(REACHES):
            p_up, p_down = fp[s, slab, 8 + k:8 + k + rows], fp[s, slab, 8 - k:8 - k + rows]
            b_up, b_down = fz[s, n, 0, slab, 8 + k:8 + k + rows], fz[s, n, 0, slab, 8 - k:8 - k + rows]
            d_up, d_down = fz[s, n, 1, slab, 8 + k:8 + k + rows], fz[s, n, 1, slab, 8 - k:8 - k + rows]
            fy[s, n, 0, slab, 0:rows] = fz[s, n, 0, slab, 8:8 + rows] + c12 * (p_up + p_down)
            fy[s, n, 1, slab, 0:rows] = b_up - b_down
            fy[s, n, 2, slab, 0:rows] = c12 * (p_up - p_down)
            fy[s, n, 3, slab, 0:rows] = 2.0 * fz[s, n, 1, slab, 8:8 + rows] + (d_up + d_down)


def force(fp, fz, fy, slab, r0, rows):
    here, inner = pl.ds(r0, rows), pl.ds(r0 + 8, rows)
    near, far = [], []
    for s in range(2):
        for n, out in enumerate((near, far)):
            k = n + 1
            gx = fy[s, n, 0, slab + k, here] - fy[s, n, 0, slab - k, here]
            gy = fy[s, n, 1, slab, here] + (fy[s, n, 2, slab + k, here] + fy[s, n, 2, slab - k, here])
            gz = fy[s, n, 3, slab, here] + (fz[s, n, 1, slab + k, inner] + fz[s, n, 1, slab - k, inner])
            out.append((gx, gy, gz))
    result = []
    for s in range(2):
        minus = -fp[s, slab, inner]
        result.append([minus * (near[1 - s][a] + far[s][a]) for a in range(3)])
    return result


def populations(s, rho, v, f, old=None):
    w = 1.0 / 36.0
    rt = (w * TAU_INV[s]) * rho
    vv = v[0] * v[0] + v[1] * v[1] + v[2] * v[2]
    vf = v[0] * f[0] + v[1] * f[1] + v[2] * f[2]
    a0 = rt * (1.0 - 1.5 * vv) - (3.0 * SRC[s] * w) * vf
    b = [3.0 * (rt * v[a] + (SRC[s] * w) * f[a]) for a in range(3)]
    g = [4.5 * rt * v[a] + (9.0 * SRC[s] * w) * f[a] for a in range(3)]
    diag = [v[a] * g[a] for a in range(3)]
    off = {(a, c): v[a] * g[c] + v[c] * g[a] for a, c in ((0, 1), (0, 2), (1, 2))}
    if old is not None:
        part = 1.0 - TAU_INV[s]
        ro = (w * part) * rho
        uu = old[0] * old[0] + old[1] * old[1] + old[2] * old[2]
        a0 = a0 + ro * (1.0 - 1.5 * uu)
        h = [4.5 * ro * old[a] for a in range(3)]
        b = [b[a] + 3.0 * ro * old[a] for a in range(3)]
        diag = [diag[a] + old[a] * h[a] for a in range(3)]
        off = {(a, c): off[a, c] + 2.0 * (old[a] * h[c]) for a, c in off}
    post = {(0, 0, 0): 12.0 * a0}
    for a in range(3):
        even, odd = a0 + diag[a], b[a]
        unit = [0, 0, 0]
        unit[a] = 1
        post[tuple(unit)] = 2.0 * (even + odd)
        post[tuple(-q for q in unit)] = 2.0 * (even - odd)
    for a, c in off:
        base = a0 + (diag[a] + diag[c])
        for sign in (1, -1):
            even = base + off[a, c] if sign == 1 else base - off[a, c]
            odd = b[a] + b[c] if sign == 1 else b[a] - b[c]
            unit = [0, 0, 0]
            unit[a], unit[c] = 1, sign
            post[tuple(unit)] = even + odd
            post[tuple(-q for q in unit)] = even - odd
    return post


def compute_kernel(*refs):
    parts, out_ref, held, load_sem = refs[:10], refs[10], refs[11:21], refs[21]
    loads = [pltpu.make_async_copy(a, b, load_sem.at[n]) for n, (a, b) in enumerate(zip(parts, held))]
    for load in loads:
        load.start()
    for load in loads:
        load.wait()
    compute_parts(*held, out_ref, *refs[22:])


def compute_parts(ro, uo, rx, ux, ry, uy, re, ue, zf, ze, out_ref,
                  rho, vel, zr, fp, fz, fy, pops, qs, qz, rho1, mom, kept, sout, outx, sem):
    for e in range(20):
        dx, x = (0, e + 2) if e < 6 else (1, e - 6) if e < 14 else (2, e - 14)
        for c in range(2):
            for j in range(4):
                if dx == 1:
                    r0 = 6 * x
                    part = (ry[0, c, r0:r0 + 6] if j == 0 else ry[1, c, r0:r0 + 6] if j == 3 else
                            ro[c, j - 1, r0:r0 + 6])
                else:
                    sx = dx // 2
                    r0 = 6 * x - (8 if sx == 0 else 0)
                    part = (re[sx, 0, c, r0:r0 + 6] if j == 0 else re[sx, 1, c, r0:r0 + 6] if j == 3 else
                            rx[sx, c, j - 1, r0:r0 + 6])
                rho[c, e, 6 * j:6 * j + 6, :] = part
    for k in range(16):
        dx, x = (0, k + 4) if k < 4 else (1, k - 4) if k < 12 else (2, k - 12)
        for f in range(3):
            for j in range(5):
                if dx == 1:
                    r0 = 4 * x
                    part = (uy[0, f, r0:r0 + 4] if j == 0 else uy[1, f, r0:r0 + 4] if j == 4 else
                            uo[f, j - 1, r0:r0 + 4])
                else:
                    sx = dx // 2
                    r0 = 4 * x - (16 if sx == 0 else 0)
                    part = (ue[sx, 0, f, r0:r0 + 4] if j == 0 else ue[sx, 1, f, r0:r0 + 4] if j == 4 else
                            ux[sx, f, j - 1, r0:r0 + 4])
                vel[f, k, 2 + 4 * j:6 + 4 * j, :] = part
    for zs in range(2):
        for dx in range(3):
            for k in range(2):
                zr[zs, dx, k, 0:6] = ze[zs, dx, 0, k, 0:6]
                zr[zs, dx, k, 6:12] = zf[zs, dx, 0, k, 0:6]
                zr[zs, dx, k, 12:18] = zf[zs, dx, 1, k, 0:6]
                zr[zs, dx, k, 18:24] = ze[zs, dx, 1, k, 0:6]
    lane = lane_of(24)
    in_seg = lane % 18
    for f in range(5):
        merged = []
        for zs in range(2):
            m = jnp.zeros((24, 128), F32)
            for dx, (e_lo, e_hi) in enumerate(((0, 6), (6, 14), (14, 20))):
                off = 6 + 8 * (dx - 1)
                for x_lo, x_hi in ((0, 4), (4, 8)) if f == 4 else ((0, 8),):
                    a, b = max(e_lo, x_lo + off), min(e_hi, x_hi + off)
                    if a >= b:
                        continue
                    tile, l0 = z_place(f, x_lo)
                    shift = 6 * (x_lo + off) - l0
                    m = jnp.where((lane >= 6 * a) & (lane < 6 * b), lroll(zr[zs, dx, tile], shift), m)
            merged.append(m)
        for xo in range(3):
            low = lroll(merged[0], -6 * xo)
            high = lroll(merged[1], 6 - 6 * xo)
            for seg in range(7):
                e = 3 * seg + xo
                if f < 2:
                    if e > 19:
                        continue
                    val = rho[f, e]
                else:
                    if e < 2 or e > 17:
                        continue
                    val = vel[f - 2, e - 2]
                val = lroll(val, 18 * seg + 6)
                low = jnp.where((lane >= 18 * seg + 6) & (lane < 18 * seg + 18), val, low)
                start = (18 * seg - 6) % 128
                if seg == 0:
                    high = jnp.where((lane >= 122) | (lane < 6), val, high)
                else:
                    high = jnp.where((lane >= start) & (lane < start + 12), val, high)
            if f < 2:
                for base, v in ((20, low), (27, high)):
                    rho[f, base + 2 + xo] = v
                    if xo == 0:
                        rho[f, base + 5] = lroll(v, -18)
                    if xo == 1:
                        rho[f, base] = lroll(v, 18)
                        rho[f, base + 6] = lroll(v, -18)
                    if xo == 2:
                        rho[f, base + 1] = lroll(v, 18)
            else:
                vel[f - 2, 16 + xo] = low
                vel[f - 2, 19 + xo] = high

    @pl.loop(0, NS1, unroll=34)
    def _(slab):
        stage_z(rho, slab, fp, fz, 8)

    @pl.loop(0, NS1, unroll=34)
    def _(slab):
        stage_y(slab, fp, fz, fy, 24)

    @pl.loop(0, 66, unroll=66)
    def _(i):
        j = i // 3
        r0 = pl.multiple_of(8 * (i - 3 * j), 8)
        here, inner = pl.ds(r0, 8), pl.ds(r0 + 8, 8)
        late, later = (j >= 16).astype(jnp.int32), (j >= 19).astype(jnp.int32)
        slab = j + 2 + 4 * late + 4 * later
        dst = j + late + 2 * later
        fs = force(fp, fz, fy, slab, r0, 8)
        r = [rho[s, slab, here] for s in range(2)]
        u = [vel[a, j, here] for a in range(3)]
        half = 0.5 / (r[0] + r[1])
        v = [u[a] + half * (fs[0][a] + fs[1][a]) for a in range(3)]
        zsum = {}
        for s in range(2):
            post = populations(s, r[s], v, fs[s], u if s == 1 else None)
            sums = {}
            for i, (cx, cy, cz) in enumerate(VELS):
                val = lroll(post[VELS[i]], cz)
                if s == 1:
                    pops[i, dst, inner] = val
                sums[cx, cy] = val if (cx, cy) not in sums else sums[cx, cy] + val
                if cz:
                    part = val if cz == 1 else -val
                    zsum[cx, cy] = part if (cx, cy) not in zsum else zsum[cx, cy] + part
            for n, key in enumerate(GROUPS):
                qs[s, n, dst, inner] = sums[key]
        for n, key in enumerate(ZGROUPS):
            qz[n, dst, inner] = zsum[key]

    for base in (16, 21):
        for n, (cx, cy) in enumerate(GROUPS):
            for s in range(2):
                if cx == 1:
                    qs[s, n, base, 8:32] = lroll(qs[s, n, base + 3, 8:32], 18)
                if cx == -1:
                    qs[s, n, base + 4, 8:32] = lroll(qs[s, n, base + 1, 8:32], -18)
        for n, (cx, cy) in enumerate(ZGROUPS):
            if cx == 1:
                qz[n, base, 8:32] = lroll(qz[n, base + 3, 8:32], 18)
            if cx == -1:
                qz[n, base + 4, 8:32] = lroll(qz[n, base + 1, 8:32], -18)
        for i, (cx, cy, cz) in enumerate(VELS):
            if cx == 1:
                pops[i, base, 8:32] = lroll(pops[i, base + 3, 8:32], 18)
            if cx == -1:
                pops[i, base + 4, 8:32] = lroll(pops[i, base + 1, 8:32], -18)

    @pl.loop(0, 20, unroll=20)
    def _(g):
        late, later = (g >= 14).astype(jnp.int32), (g >= 17).astype(jnp.int32)
        src = g + 1 + 2 * late + 2 * later
        dst = g + 2 * late + 4 * later
        mx = my = 0.0
        for s in range(2):
            top = bottom = 0.0
            for n, (cx, cy) in enumerate(GROUPS):
                a = qs[s, n, src - cx, 13 - cy:29 - cy]
                top = top + a
                bottom = bottom + qs[s, n, src - cx, 5 - cy:13 - cy]
                mx = mx + cx * a if cx else mx
                my = my + cy * a if cy else my
            rho1[s, dst, 8:24] = top
            rho1[s, dst, 0:8] = bottom
        mz = 0.0
        for n, (cx, cy) in enumerate(ZGROUPS):
            mz = mz + qz[n, src - cx, 13 - cy:29 - cy]
        mom[0, dst], mom[1, dst], mom[2, dst] = mx, my, mz

    for base in (14, 21):
        for s in range(2):
            rho1[s, base] = lroll(rho1[s, base + 3], 18)
            rho1[s, base + 1] = lroll(rho1[s, base + 4], 18)
            rho1[s, base + 5] = lroll(rho1[s, base + 2], -18)
            rho1[s, base + 6] = lroll(rho1[s, base + 3], -18)

    @pl.loop(0, NS2, unroll=28)
    def _(slab):
        stage_z(rho1, slab, fp, fz, 0)

    @pl.loop(0, NS2, unroll=28)
    def _(slab):
        stage_y(slab, fp, fz, fy, 16)

    def motion(slab, r0):
        here, inner = pl.ds(r0, 8), pl.ds(r0 + 8, 8)
        fs = force(fp, fz, fy, slab, r0, 8)
        inv = 1.0 / (rho1[0, slab, inner] + rho1[1, slab, inner])
        return [(mom[a, slab, here] + 0.5 * (fs[0][a] + fs[1][a])) * inv for a in range(3)], fs

    def second(s, slab, src, r0, v, f, write):
        post = populations(s, rho1[s, slab, pl.ds(r0 + 8, 8)], v, f)
        for i, (cx, cy, cz) in enumerate(VELS):
            val = post[VELS[i]]
            if s == 1:
                val = val - 0.25 * pops[i, src - cx, pl.ds(r0 + 13 - cy, 8)]
            write(i, lroll(val, cz))

    @pl.loop(0, 6, unroll=6)
    def _(t):
        later = (t >= 3).astype(jnp.int32)
        for r0 in (0, 8):
            v, fs = motion(16 + t + 4 * later, r0)
            for s in range(2):
                def write(i, val):
                    sout[s, i, t, r0:r0 + 8] = val

                second(s, 16 + t + 4 * later, 17 + t + 2 * later, r0, v, fs[s], write)

    lane8 = lane_of(8)
    seg8 = lane8 % 18
    from_low = (seg8 >= 6) & (seg8 < 12)
    edge = (lane8 < 6) | (lane8 >= 122)

    def finish(s, k, r0, v, f):
        e = k + 5
        seg = e // 3
        xo = e - 3 * seg
        shift = lax.rem(256 - 18 * seg - 6, 128)

        def write(i, val):
            strip = jnp.where(from_low, sout[s, i, xo, r0:r0 + 8], sout[s, i, xo + 3, r0:r0 + 8])
            val = jnp.where(edge, pltpu.roll(strip, shift, 1), val)
            x = k - 1 + VELS[i][0]
            first = jnp.where((x >= 0) & (x < 8), 8 * (VELS[i][1] + 1) + x, 144)
            outx[s, i, pl.ds(first + 8 * r0, 8, stride=8)] = val

        second(s, k + 2, k + 3, r0, v, f, write)

    @pl.loop(0, 10, unroll=10)
    def _(k):
        for r0 in (0, 8):
            v, fs = motion(k + 2, r0)
            for a in range(3):
                kept[a, k, r0:r0 + 8] = v[a]
                kept[3 + a, k, r0:r0 + 8] = fs[1][a]
            finish(0, k, r0, v, fs[0])

    first = pltpu.make_async_copy(outx.at[0, :, 16:112], out_ref.at[0], sem.at[0])
    first.start()

    @pl.loop(0, 10, unroll=10)
    def _(k):
        for r0 in (0, 8):
            finish(1, k, r0, [kept[a, k, r0:r0 + 8] for a in range(3)], [kept[3 + a, k, r0:r0 + 8] for a in range(3)])

    second_half = pltpu.make_async_copy(outx.at[1, :, 16:112], out_ref.at[1], sem.at[1])
    second_half.start()
    first.wait()
    second_half.wait()


def compute(parts):
    anywhere = pl.BlockSpec(memory_space=pl.ANY)
    return pl.pallas_call(
        compute_kernel,
        out_shape=jax.ShapeDtypeStruct((2, 19, 96, 128), F32),
        in_specs=[anywhere] * len(parts),
        out_specs=anywhere,
        scratch_shapes=[pltpu.VMEM(part.shape, F32) for part in parts] + [
            pltpu.SemaphoreType.DMA((len(parts),)), pltpu.VMEM((2, NS1, 24, 128), F32), pltpu.VMEM((3, 22, 24, 128), F32), pltpu.VMEM((2, 3, 2, 24, 128), F32),
            pltpu.VMEM((2, NS1, 40, 128), F32), pltpu.VMEM((2, 2, 2, NS1, 40, 128), F32),
            pltpu.VMEM((2, 2, 4, NS1, 24, 128), F32), pltpu.VMEM((19, NP1, 40, 128), F32),
            pltpu.VMEM((2, 9, NP1, 40, 128), F32), pltpu.VMEM((5, NP1, 40, 128), F32),
            pltpu.VMEM((2, NS2, 24, 128), F32), pltpu.VMEM((3, NS2, 16, 128), F32),
            pltpu.VMEM((6, 10, 16, 128), F32),
            pltpu.VMEM((2, 19, 6, 16, 128), F32),
            pltpu.VMEM((2, 19, 272, 128), F32), pltpu.SemaphoreType.DMA((2,))],
        compiler_params=pltpu.CompilerParams(vmem_limit_bytes=60 << 20),
    )(*parts)


def local(labels, density_jitter, velocity):
    rows = [jnp.swapaxes(a, -3, -2).reshape(a.shape[:-3] + (96, 128)) for a in (labels, density_jitter, velocity)]
    out = compute(exchange(*rows))
    return jnp.swapaxes(out.reshape(2, 19, 12, 8, 128), 2, 3)


def solution(mesh):
    in_specs = (P("gx", "gy", "gz"), P(None, "gx", "gy", "gz"), P(None, "gx", "gy", "gz"))
    out_specs = P(None, None, "gx", "gy", "gz")
    return jax.shard_map(local, mesh=mesh, in_specs=in_specs, out_specs=out_specs, check_vma=False)
```
